512 devices in a mesh: wide: 64 (over z, x_hi, core), narrow: 8 (over y, x_lo).
Axes of the slice: x: 4 (x_hi: 2, x_lo: 2; x = x_hi * 2 + x_lo), y: 4, z: 16, core: 2. Of those that a mesh axis runs over, the one named last changes fastest.
Arguments:
- panels: bfloat16 [64, 8192, 128], P('wide', 'narrow'), may hold values from -6 to 6
- stiff_blocks: bfloat16 [64, 1216, 4096], P('wide', 'narrow'), may hold values from -0.375 to 0.375
- mass_blocks: bfloat16 [64, 1216, 4096], P('wide', 'narrow'), may hold values from -0.375 to 0.375
- block_rows: int32 [64, 1216], P('wide', 'narrow'), may hold values from 0 to 16, as said below
- block_cols: int32 [64, 1216], P('wide', 'narrow'), may hold values from 0 to 127
- interface_map: int32 [64, 8192], P('wide', 'narrow'), may hold values from 0 to 8191, as said below
- cond_vectors: bfloat16 [8192, 768], P('narrow'), may hold values from -0.1875 to 0.1875
Outputs:
- condensed: bfloat16 [64, 8, 768, 512], P('wide', 'narrow')
The draws below stay inside these ranges and needn't reach their ends.
Inputs may be any that keep to these rules, and one draw needn't show every extreme that they name: `block_rows`: in each partition's 152 slots the used slots come first; on some partition all 152 are used. `interface_map`: for every cell a permutation of the rows; of the 1024 rows of one partition at most 256 land in any one interface group, and in every cell some partition sends exactly 256 to some group.
All inputs are finite; a program needn't handle non-finite values.
Results may differ from the reference program's by a relative error of at most 0.0049.
Values may be sent and summed in bfloat16 or wider, within the bound.
A program may use at most 128 MiB of HBM per device.

```python
import jax
import jax.numpy as jnp
from jax import lax

BLK = 64
PC = 128
NC = 768
RB_DEV = 16
SLOTS_DEV = 152
ROWS_DEV = 1024
CELLS = 64
CELL_BLOCKS = 128
CELL_DOF = 8192
SLOTS = 1216
PEER_CAP = 256


def draw_block_rows(key, part):
    device_count = CELLS * (SLOTS // SLOTS_DEV)
    key_count, key_full, key_rows = jax.random.split(key, 3)
    used_count = SLOTS_DEV // (1 + jax.random.randint(key_count, (device_count,), 0, 4))
    full_device = jax.random.randint(key_full, (), 0, device_count)
    used_count = jnp.where(jnp.arange(device_count) == full_device, SLOTS_DEV, used_count)
    row_values = jax.random.randint(key_rows, (device_count, SLOTS_DEV), 0, RB_DEV)
    used_slots = jnp.arange(SLOTS_DEV)[None, :] < used_count[:, None]
    return jnp.where(used_slots, row_values, RB_DEV).reshape(CELLS, SLOTS).astype(jnp.int32)


def draw_interface_map(key, part):
    group_count = CELL_DOF // ROWS_DEV
    half_groups = group_count // 2

    def one_cell(cell_key):
        key_offsets, key_slots, key_rows = jax.random.split(cell_key, 3)
        offsets = jax.random.permutation(key_offsets, group_count)[:half_groups]
        source = jnp.broadcast_to(jnp.arange(group_count)[:, None], (group_count, ROWS_DEV))
        row_index = jnp.broadcast_to(jnp.arange(ROWS_DEV)[None, :], (group_count, ROWS_DEV))
        offset_rank = row_index // PEER_CAP
        target = (source + offsets[offset_rank]) % group_count
        slot_index = offset_rank * PEER_CAP + row_index % PEER_CAP
        slot_perms = jax.vmap(lambda k: jax.random.permutation(k, ROWS_DEV))(jax.random.split(key_slots, group_count))
        position = target * ROWS_DEV + slot_perms[target, slot_index]
        row_perms = jax.vmap(lambda k: jax.random.permutation(k, ROWS_DEV))(jax.random.split(key_rows, group_count))
        result = jnp.zeros((group_count, ROWS_DEV), jnp.int32).at[source, row_perms].set(position.astype(jnp.int32))
        return result.reshape(CELL_DOF)
    return jax.vmap(one_cell)(jax.random.split(key, CELLS)).astype(jnp.int32)


def with_ends(values, own_key, least, top_value):
    shape = values.shape
    place = [jax.random.randint(jax.random.fold_in(own_key, axis), (), 0, shape[axis]) for axis in range(len(shape))]
    values = values.at[tuple(place)].set(least)
    longest = shape.index(max(shape))
    place[longest] = (place[longest] + 1) % shape[longest]
    return values.at[tuple(place)].set(top_value)


def steps_of(own_key, shape, cuts, smallest, high):
    def one(dim, parts):
        heights = jax.random.uniform(jax.random.fold_in(jax.random.fold_in(own_key, 6), dim), (parts,), jnp.float32, smallest / len(cuts), high / len(cuts))
        return jnp.repeat(jnp.exp(heights), shape[dim] // parts).reshape((-1,) + (1,) * (len(shape) - dim - 1))

    gain = one(*cuts[0])
    for cut in cuts[1:]:
        gain = gain * one(*cut)
    return gain


def noise(rng, shape, spread, bound, cuts=(), held_as=jnp.bfloat16):
    entries = spread * jax.random.normal(rng, shape, jnp.float32)
    if cuts:
        entries = entries * steps_of(rng, shape, cuts, -0.22, 0.18)
    return jnp.clip(entries, -bound, bound).astype(held_as)


def setup_inputs(seed: int = 0) -> dict:
    arg_keys = jax.random.split(jax.random.key(seed), 8)
    return {
        "panels": noise(arg_keys[0], (CELLS, CELL_DOF, PC), 1.0, 6.0, ((0, 64), (1, 8))),
        "stiff_blocks": noise(arg_keys[1], (CELLS, SLOTS, BLK * BLK), (4 * BLK) ** -0.5, 0.375, ((0, 64), (1, 8))),
        "mass_blocks": noise(arg_keys[2], (CELLS, SLOTS, BLK * BLK), (4 * BLK) ** -0.5, 0.375, ((0, 64), (1, 8))),
        "block_rows": draw_block_rows(jax.random.fold_in(arg_keys[7], 71), 0),
        "block_cols": with_ends(jax.random.randint(arg_keys[4], (CELLS, SLOTS), 0, CELL_BLOCKS), jax.random.fold_in(arg_keys[4], 1), 0, CELL_BLOCKS - 1).astype(jnp.int32),
        "interface_map": draw_interface_map(jax.random.fold_in(arg_keys[7], 71), 0),
        "cond_vectors": noise(arg_keys[6], (CELL_DOF, NC), ROWS_DEV ** -0.5, 0.1875, ((0, 8),)),
    }


def reference(panels, stiff_blocks, mass_blocks, block_rows, block_cols, interface_map, cond_vectors):
    group_count = CELL_DOF // ROWS_DEV
    chosen = [panels[0], panels[CELLS // 2]]
    slot_group = (jnp.arange(SLOTS) // SLOTS_DEV).astype(jnp.int32)

    def one_cell(cell_args):
        stiffness, mass_matrix, row_index, column_index, row_map = cell_args
        global_row = jnp.where(row_index < RB_DEV, slot_group * RB_DEV + row_index, CELL_BLOCKS).astype(jnp.int32)
        stiffness = stiffness.reshape(SLOTS, BLK, BLK).astype(jnp.float32)
        mass_matrix = mass_matrix.reshape(SLOTS, BLK, BLK).astype(jnp.float32)
        pieces = []
        for panel_cols in chosen:
            blocks = panel_cols.reshape(CELL_BLOCKS, BLK, PC)[column_index].astype(jnp.float32)
            for matrix in (stiffness, mass_matrix):
                product = jnp.einsum('sij,sjc->sic', matrix, blocks, precision=lax.Precision.HIGHEST)
                summed = jax.ops.segment_sum(product, global_row, num_segments=CELL_BLOCKS + 1)[:CELL_BLOCKS]
                pieces.append(summed.reshape(CELL_DOF, PC))
        product_rows = jnp.concatenate(pieces, axis=1).astype(jnp.bfloat16)
        regrouped = jnp.zeros_like(product_rows).at[row_map].set(product_rows)
        per_group = regrouped.reshape(group_count, ROWS_DEV, 4 * PC).astype(jnp.float32)
        vectors = cond_vectors.reshape(group_count, ROWS_DEV, NC).astype(jnp.float32)
        condensed = jnp.einsum('grn,grc->gnc', vectors, per_group, precision=lax.Precision.HIGHEST)
        return condensed.astype(jnp.bfloat16)

    return lax.map(one_cell, (stiff_blocks, mass_blocks, block_rows, block_cols, interface_map))
```

```python
import jax
import jax.numpy as jnp
from jax import lax
from jax.experimental import pallas as pl
from jax.experimental.pallas import tpu as pltpu
from jax.sharding import PartitionSpec as P

BLK = 64
PC = 128
NC = 768
RB = 16
SLOTS = 152
ROWS = 1024
CAP = 256
GROUPS = 52
SORTED = GROUPS * 4
F32 = jnp.float32
BF16 = jnp.bfloat16


def iota(shape, dim):
    return lax.broadcasted_iota(jnp.int32, shape, dim)


def kernel(
    pan_in, stiff, mass, brow, bcol, imap, vec, out,
    own, other, kx, mx, vx, vt, perm, zk, zm, lhs, run, prod, sel, wts, pos_s, pos_r, send, recv,
    meta, meta_s,
    load_sem, meta_sem, a_send, a_recv, f_send, b1_send, b1_recv, b2_send, b2_recv,
    c_send, c_recv, p_send, p_recv, x_send, x_recv,
):
    w = lax.axis_index("wide")
    n = lax.axis_index("narrow")
    core = lax.rem(w, 2)
    xh = lax.rem(w // 2, 2)
    z = w // 4
    y = n // 2
    xl = lax.rem(n, 2)
    x = 2 * xh + xl

    def dev(z_, xh_, core_, n_):
        return {"wide": z_ * 4 + xh_ * 2 + core_, "narrow": n_}

    def remote(src, dst, ssem, rsem, where):
        return pltpu.make_async_remote_copy(
            src_ref=src, dst_ref=dst, send_sem=ssem, recv_sem=rsem,
            device_id=where, device_id_type=pl.DeviceIdType.MESH,
        )

    loads = [
        pltpu.make_async_copy(stiff.at[0], kx, load_sem.at[0]),
        pltpu.make_async_copy(mass.at[0], mx, load_sem.at[1]),
        pltpu.make_async_copy(vec, vx, load_sem.at[2]),
    ]
    for c in loads:
        c.start()

    def narrow_peer(d):
        return dev(z, xh, core, lax.rem(y + d // 2, 4) * 2 + lax.rem(xl + d % 2, 2))

    def x_at(xx):
        return dev(z, xx // 2, core, y * 2 + lax.rem(xx, 2))

    def y_at(yy):
        return dev(z, xh, core, yy * 2 + xl)

    sibling = dev(z, xh, 1 - core, n)
    zm4 = lax.rem(z, 4)
    is_mid = zm4 == 0
    owner = z // 8
    is_src = jnp.logical_and(lax.rem(z, 8) == 0, jnp.logical_and(xh == 0, core == 0))
    src_z = 8 * core

    def up(d):
        return dev(lax.rem(z + 16 + d, 16), xh, core, n)

    STEPS = (2, 1, -1)
    middle = dev(lax.rem(jnp.where(zm4 == 3, z + 1, z - zm4), 16), xh, core, n)

    barrier = pltpu.get_barrier_semaphore()

    def greet(where):
        pl.semaphore_signal(barrier, inc=1, device_id=where, device_id_type=pl.DeviceIdType.MESH)

    for d in range(1, 8):
        greet(narrow_peer(d))
    greet(x_at(lax.rem(x + 2, 4)))
    greet(x_at(lax.rem(jnp.where(xl == 0, x + 3, x + 1), 4)))
    greet(sibling)

    @pl.when(is_mid)
    def _():
        for d in STEPS:
            greet(up(d))

    @pl.when(jnp.logical_not(is_mid))
    def _():
        greet(middle)

    is_self = jnp.logical_and(is_src, owner == 0)

    @pl.when(is_src)
    def _():
        for k in range(4):
            for h in range(2):
                if (k, h) != (0, 0):
                    greet(dev(lax.rem(z + 4 * k, 16), h, owner, n))

        @pl.when(owner == 1)
        def _():
            greet(sibling)

    is_fed = jnp.logical_and(is_mid, jnp.logical_not(is_self))

    @pl.when(is_fed)
    def _():
        greet(dev(src_z, 0, 0, n))

    pl.semaphore_wait(
        barrier,
        10
        + jnp.where(is_mid, 3, 1)
        + jnp.where(is_src, 7 + owner, 0)
        + jnp.where(is_fed, 1, 0),
    )

    def a_rows(yy, xx):
        return pl.ds(yy * 16 + xx * 4, 4)

    def b_rows(yy, xx):
        return pl.ds(64 + xx * 16 + yy * 4, 4)

    mine_a = own.at[a_rows(y, x)]
    mine_b = own.at[b_rows(y, x)]

    @pl.when(is_src)
    def _():
        for i, rows in enumerate((a_rows, b_rows)):
            for k in (2, 1, 3, 0):
                for h in range(2):
                    src = pan_in.at[pl.ds(h * 8 + i * 4, 4)]
                    dst = own.at[rows(y, 2 * h + xl)]
                    s = a_send.at[i, k * 2 + h]
                    if (k, h) != (0, 0):
                        remote(src, dst, s, a_recv.at[i], dev(lax.rem(z + 4 * k, 16), h, owner, n)).start()
                    else:
                        @pl.when(owner == 0)
                        def _():
                            pltpu.make_async_copy(src, dst, a_recv.at[i]).start()

                        @pl.when(owner == 1)
                        def _():
                            remote(src, dst, s, a_recv.at[i], sibling).start()

    m = imap[...]
    target = lax.shift_right_logical(m, 10)
    spot = jnp.bitwise_and(m, 1023) + 1
    tri = jnp.where(iota((128, 128), 0) < iota((128, 128), 1), 1.0, 0.0).astype(BF16)
    carry = jnp.zeros((8, 1), F32)
    idx_parts = []
    for b in range(8):
        tb = target[:, b * 128 : (b + 1) * 128]
        hit = jnp.where(iota((8, 128), 0) == jnp.broadcast_to(tb, (8, 128)), 1.0, 0.0)
        before = jnp.dot(hit.astype(BF16), tri, preferred_element_type=F32) + carry
        carry = carry + jnp.sum(hit, axis=1, keepdims=True)
        rank = jnp.sum(hit * before, axis=0, keepdims=True)
        idx_parts.append(tb * CAP + rank.astype(jnp.int32))
    idx = jnp.concatenate(idx_parts, axis=1)
    spot8 = jnp.broadcast_to(spot, (8, ROWS))
    hi = lax.shift_right_logical(spot8, 5)
    lo = jnp.bitwise_and(spot8, 31)
    two = jnp.where(iota((8, ROWS), 0) == 0, hi, lo).astype(F32).astype(BF16)

    def build(g, _):
        rows = pl.ds(pl.multiple_of(g * CAP, CAP), CAP)
        s = jnp.where(iota((CAP, ROWS), 0) + g * CAP == idx, 1.0, 0.0).astype(BF16)
        sel[rows, :] = s
        t = lax.dot_general(two, s, (((1,), (1,)), ((), ())), preferred_element_type=F32)
        pos_s[g] = t
        return 0

    lax.fori_loop(0, 8, build, 0)

    pos_out = []
    for d in range(1, 8):
        to = lax.rem(y + d // 2, 4) * 2 + lax.rem(xl + d % 2, 2)
        c = remote(pos_s.at[to], pos_r.at[d], p_send.at[d], p_recv.at[d], narrow_peer(d))
        c.start()
        pos_out.append(c)
    pos_r[0] = pos_s[n]

    f_out, b1_out, b1_in = [], [], []
    fed = (
        remote(mine_a, mine_a, a_send.at[0, 0], a_recv.at[0], sibling),
        remote(mine_b, mine_b, a_send.at[1, 0], a_recv.at[1], sibling),
    )
    for i, mine in enumerate((mine_a, mine_b)):
        fed[i].wait_recv()

        @pl.when(is_mid)
        def _():
            for k, d in enumerate(STEPS):
                remote(mine, mine, f_send.at[i, k], a_recv.at[i], up(d)).start()

        for d in (2, 1, 3):
            if i == 0:
                to, came = x_at(lax.rem(x + d, 4)), own.at[a_rows(y, lax.rem(x + 4 - d, 4))]
            else:
                to, came = y_at(lax.rem(y + d, 4)), own.at[b_rows(lax.rem(y + 4 - d, 4), x)]
            c = remote(mine, mine, b1_send.at[i, d], b1_recv.at[i, d], to)
            c.start()
            b1_out.append(c)
            b1_in.append(remote(came, came, b1_send.at[i, d], b1_recv.at[i, d], to))

    br = brow[...]
    bc = bcol[...]
    sq = (SLOTS, SLOTS)
    diag = iota(sq, 0) == iota(sq, 1)
    br_b = jnp.broadcast_to(br, sq)
    brc = jnp.sum(jnp.where(diag, br_b, 0), axis=1, keepdims=True)
    bcc = jnp.sum(jnp.where(diag, jnp.broadcast_to(bc, sq), 0), axis=1, keepdims=True)
    earlier = jnp.logical_and(iota(sq, 0) < iota(sq, 1), brc == br_b)
    rank = jnp.sum(jnp.where(earlier, 1, 0), axis=0, keepdims=True)
    same = iota((RB, SLOTS), 0) == jnp.broadcast_to(br, (RB, SLOTS))
    count = jnp.sum(jnp.where(same, 1, 0), axis=1, keepdims=True)
    padded = jnp.bitwise_and(count + 3, -4)
    off = jnp.sum(jnp.where(iota((RB, SLOTS), 0) < br, padded, 0), axis=0, keepdims=True)
    dest = jnp.where(br < RB, off + rank, 4096)
    destc = jnp.sum(jnp.where(diag, jnp.broadcast_to(dest, sq), 0), axis=1, keepdims=True)
    count_l = jnp.sum(jnp.where(brc == iota((SLOTS, 128), 1), 1, 0), axis=0, keepdims=True)
    padded_l = jnp.bitwise_and(count_l + 3, -4)
    off_c = jnp.sum(jnp.where(iota((RB, 128), 1) < iota((RB, 128), 0), padded_l, 0), axis=1, keepdims=True)
    begins = jnp.logical_and(lax.shift_right_logical(off_c, 2) == iota((RB, 256), 1), count > 0)
    keep = 1 - jnp.sum(jnp.where(begins, 1, 0), axis=0, keepdims=True)
    end_l = jnp.sum(jnp.where(iota((RB, 256), 0) <= iota((RB, 256), 1), padded, 0), axis=0, keepdims=True)
    last = jnp.maximum(lax.shift_right_logical(end_l, 2) - 1, 0)
    some = jnp.minimum(count_l, 1)
    some = jnp.concatenate([some, some], axis=1)
    q = jnp.bitwise_and(bcc, 3)
    part = jnp.bitwise_and(lax.shift_right_logical(bcc, 2), 1)
    bx = 2 * jnp.bitwise_and(lax.shift_right_logical(bcc, 3), 1) + jnp.bitwise_and(lax.shift_right_logical(bcc, 4), 1)
    by = lax.shift_right_logical(bcc, 5)
    place = jnp.where(part == 1, 64 + bx * 16 + by * 4, by * 16 + bx * 4) + q
    block = jnp.sum(jnp.where(destc == iota((SLOTS, 256), 1), place, 0), axis=0, keepdims=True)
    r8 = iota((8, 256), 0)
    meta[...] = jnp.where(r8 == 0, block, jnp.where(r8 == 1, keep, jnp.where(r8 == 2, last, some)))
    to_scalar = pltpu.make_async_copy(meta, meta_s, meta_sem)
    to_scalar.start()
    perm[...] = jnp.where(iota((SORTED, SLOTS), 0) == dest, 1.0, 0.0).astype(BF16)

    for c in b1_in:
        c.wait_recv()
    row_a = own.at[pl.ds(y * 16, 16)]
    row_b = own.at[pl.ds(64 + x * 16, 16)]
    far_a = other.at[pl.ds(y * 16, 16)]
    far_b = other.at[pl.ds(64 + x * 16, 16)]
    b2_out, b2_in, c_out = [], [], []
    for d in (2, 1, 3):
        for i in range(2):
            if i == 0:
                to, o = y_at(lax.rem(y + d, 4)), lax.rem(y + 4 - d, 4) * 16
            else:
                to, o = x_at(lax.rem(x + d, 4)), 64 + lax.rem(x + 4 - d, 4) * 16
            block_ref = (row_a, row_b)[i]
            c = remote(block_ref, block_ref, b2_send.at[i, d], b2_recv.at[i, d], to)
            c.start()
            b2_out.append(c)
            came = own.at[pl.ds(o, 16)]
            b2_in.append((came, o, d, remote(came, came, b2_send.at[i, d], b2_recv.at[i, d], to)))
    for i, block_ref in enumerate((row_a, row_b)):
        c = remote(block_ref, (far_a, far_b)[i], c_send.at[i], c_recv.at[i], sibling)
        c.start()
        c_out.append(c)

    loads[0].wait()
    loads[1].wait()

    def order(j, _):
        lanes = pl.ds(pl.multiple_of(j * 512, 512), 512)
        for src, dst in ((kx, zk), (mx, zm)):
            t = jnp.dot(perm[...], src[:, lanes], preferred_element_type=F32)
            for i in range(4):
                dst[pl.ds(j * 4 + i, SORTED, stride=32), :] = t[:, i * 128 : (i + 1) * 128]
        return 0

    lax.fori_loop(0, 8, order, 0)
    left = iota((32, 128), 1) < 64

    def assemble(g, _):
        for mat, src in enumerate((zk, zm)):
            for pair in range(2):
                o = pl.multiple_of(g * 128 + pair * 64, 64)
                t0 = src[pl.ds(o, 32), :]
                t1 = src[pl.ds(o + 32, 32), :]
                even = jnp.where(left, t0, pltpu.roll(t1, 64, 1))
                odd = jnp.where(left, pltpu.roll(t0, 64, 1), t1)
                lhs[g, mat * 64 : mat * 64 + 32, pair * 128 : (pair + 1) * 128] = even.astype(BF16)
                lhs[g, mat * 64 + 32 : mat * 64 + 64, pair * 128 : (pair + 1) * 128] = odd.astype(BF16)
        return 0

    lax.fori_loop(0, GROUPS, assemble, 0)

    loads[2].wait()

    def flip(k, _):
        o = pl.ds(pl.multiple_of(k * 256, 256), 256)
        vt[:, o] = vx[o, :].T
        return 0

    lax.fori_loop(0, 4, flip, 0)
    for d in range(1, 8):
        pos_out[d - 1].wait_recv()

    def weigh(d, _):
        t = pos_r[d]
        at = (t[0:1, :] * 32.0 + t[1:2, :]).astype(jnp.int32)
        q_d = jnp.where(iota((ROWS, CAP), 0) + 1 == at, 1.0, 0.0).astype(BF16)
        wts[:, pl.ds(pl.multiple_of(d * CAP, CAP), CAP)] = jnp.dot(
            vt[...], q_d, preferred_element_type=F32
        ).astype(BF16)
        return 0

    lax.fori_loop(0, 8, weigh, 0)

    for k, (came, o, d, c) in enumerate(b2_in):
        c.wait_recv()
        h = remote(came, other.at[pl.ds(o, 16)], c_send.at[2 + k], c_recv.at[2 + k], sibling)
        h.start()
        c_out.append(h)
    to_scalar.wait()

    x_out, x_in = [], []
    for half in range(2):
        pan = (own, other)[half]
        if half == 1:
            offs = [y * 16, 64 + x * 16] + [o for _, o, _, _ in b2_in]
            for k, o in enumerate(offs):
                came = other.at[pl.ds(o, 16)]
                remote(came, came, c_send.at[k], c_recv.at[k], sibling).wait_recv()

        def multiply(g, held):
            rhs = jnp.concatenate(
                [
                    pan[meta_s[0, g * 4 + i]]
                    for i in range(4)
                ],
                axis=0,
            )
            t = jnp.dot(lhs[g], rhs, preferred_element_type=F32)
            held = t + held * meta_s[1, g].astype(F32)
            run[g] = held
            return held

        lax.fori_loop(0, GROUPS, multiply, jnp.zeros((128, PC), F32))

        def collect(r, _):
            t = run[meta_s[2, r]] * meta_s[3, r].astype(F32)
            rows = pl.ds(pl.multiple_of(r * BLK, BLK), BLK)
            prod[rows, 0:PC] = t[0:BLK].astype(BF16)
            prod[rows, PC : 2 * PC] = t[BLK : 2 * BLK].astype(BF16)
            return 0

        lax.fori_loop(0, RB, collect, 0)

        for d in (4, 5, 2, 3, 6, 7, 1, 0):
            to = lax.rem(y + d // 2, 4) * 2 + lax.rem(xl + d % 2, 2)
            rows = pl.ds(pl.multiple_of(to * CAP, CAP), CAP)
            t = jnp.dot(sel[rows, :], prod[...], preferred_element_type=F32).astype(BF16)
            if d == 0:
                recv[half, 0:CAP, :] = t
            else:
                send[half, d] = t
                c = remote(
                    send.at[half, d], recv.at[half, d * CAP : (d + 1) * CAP],
                    x_send.at[half, d], x_recv.at[half, d], narrow_peer(d),
                )
                c.start()
                x_out.append(c)

    for half in range(2):
        which = core if half == 0 else 1 - core
        for c in x_out[half * 7 : half * 7 + 7]:
            c.wait_recv()
        t = jnp.dot(wts[...], recv[half], preferred_element_type=F32)
        out[:, pl.ds(pl.multiple_of(which * 2 * PC, 2 * PC), 2 * PC)] = t.astype(BF16)

    for c in pos_out + b1_out + b2_out + c_out + x_out:
        c.wait_send()

    @pl.when(is_mid)
    def _():
        for i, mine in enumerate((mine_a, mine_b)):
            for k, d in enumerate(STEPS):
                remote(mine, mine, f_send.at[i, k], a_recv.at[i], up(d)).wait_send()

    @pl.when(is_src)
    def _():
        for i, rows in enumerate((a_rows, b_rows)):
            for k in (2, 1, 3, 0):
                for h in range(2):
                    src = pan_in.at[pl.ds(h * 8 + i * 4, 4)]
                    dst = own.at[rows(y, 2 * h + xl)]
                    s = a_send.at[i, k * 2 + h]
                    if (k, h) != (0, 0):
                        remote(src, dst, s, a_recv.at[i], dev(lax.rem(z + 4 * k, 16), h, owner, n)).wait_send()
                    else:
                        @pl.when(owner == 1)
                        def _():
                            remote(src, dst, s, a_recv.at[i], sibling).wait_send()


def body(panels, stiff_blocks, mass_blocks, block_rows, block_cols, interface_map, cond_vectors):
    places = interface_map.reshape(RB, 32, 2).transpose(0, 2, 1).reshape(1, ROWS)
    hbm = pl.BlockSpec(memory_space=pl.ANY)
    vmem = pl.BlockSpec(memory_space=pltpu.VMEM)
    dma = pltpu.SemaphoreType.DMA
    res = pl.pallas_call(
        kernel,
        out_shape=jax.ShapeDtypeStruct((NC, 4 * PC), BF16),
        in_specs=[hbm, hbm, hbm, vmem, vmem, vmem, hbm],
        out_specs=vmem,
        scratch_shapes=[
            pltpu.VMEM((128, BLK, PC), BF16),
            pltpu.VMEM((128, BLK, PC), BF16),
            pltpu.VMEM((SLOTS, BLK * BLK), BF16),
            pltpu.VMEM((SLOTS, BLK * BLK), BF16),
            pltpu.VMEM((ROWS, NC), BF16),
            pltpu.VMEM((NC, ROWS), BF16),
            pltpu.VMEM((SORTED, SLOTS), BF16),
            pltpu.VMEM((SORTED * 32, 128), F32),
            pltpu.VMEM((SORTED * 32, 128), F32),
            pltpu.VMEM((GROUPS, 128, 256), BF16),
            pltpu.VMEM((GROUPS, 128, PC), F32),
            pltpu.VMEM((ROWS, 2 * PC), BF16),
            pltpu.VMEM((8 * CAP, ROWS), BF16),
            pltpu.VMEM((NC, 8 * CAP), BF16),
            pltpu.VMEM((8, 8, CAP), F32),
            pltpu.VMEM((8, 8, CAP), F32),
            pltpu.VMEM((2, 8, CAP, 2 * PC), BF16),
            pltpu.VMEM((2, 8 * CAP, 2 * PC), BF16),
            pltpu.VMEM((8, 256), jnp.int32),
            pltpu.SMEM((8, 256), jnp.int32),
            dma((3,)), dma, dma((2, 8)), dma((2,)), dma((2, 3)), dma((2, 4)), dma((2, 4)), dma((2, 4)), dma((2, 4)),
            dma((8,)), dma((8,)), dma((8,)), dma((8,)), dma((2, 8)), dma((2, 8)),
        ],
        compiler_params=pltpu.CompilerParams(
            collective_id=0, has_side_effects=True, vmem_limit_bytes=60 * 2**20
        ),
    )(panels.reshape(RB, BLK, PC), stiff_blocks, mass_blocks, block_rows, block_cols, places, cond_vectors)
    return res.reshape(1, 1, NC, 4 * PC)


def solution(mesh):
    return jax.shard_map(
        body,
        mesh=mesh,
        in_specs=(
            P("wide", "narrow", None),
            P("wide", "narrow", None),
            P("wide", "narrow", None),
            P("wide", "narrow"),
            P("wide", "narrow"),
            P("wide", "narrow"),
            P("narrow", None),
        ),
        out_specs=P("wide", "narrow", None, None),
        check_vma=False,
    )
```

```python
import jax
import jax.numpy as jnp
from jax import lax
from jax.experimental import pallas as pl
from jax.experimental.pallas import tpu as pltpu
from jax.sharding import PartitionSpec as P

BLK = 64
PC = 128
NC = 768
RB = 16
SLOTS = 152
ROWS = 1024
CAP = 256
GROUPS = 52
SORTED = GROUPS * 4
F32 = jnp.float32
BF16 = jnp.bfloat16


def iota(shape, dim):
    return lax.broadcasted_iota(jnp.int32, shape, dim)


def kernel(
    pan_in, stiff, mass, brow, bcol, imap, vec, out,
    own, other, kx, mx, vx, vt, perm, zk, zm, lhs, run, prod, sel, wts, pos_s, pos_r, send, recv,
    meta, meta_s,
    load_sem, meta_sem, a_send, a_recv, f_send, b1_send, b1_recv, b2_send, b2_recv,
    c_send, c_recv, p_send, p_recv, x_send, x_recv,
):
    w = lax.axis_index("wide")
    n = lax.axis_index("narrow")
    core = lax.rem(w, 2)
    xh = lax.rem(w // 2, 2)
    z = w // 4
    y = n // 2
    xl = lax.rem(n, 2)
    x = 2 * xh + xl

    def dev(z_, xh_, core_, n_):
        return {"wide": z_ * 4 + xh_ * 2 + core_, "narrow": n_}

    def remote(src, dst, ssem, rsem, where):
        return pltpu.make_async_remote_copy(
            src_ref=src, dst_ref=dst, send_sem=ssem, recv_sem=rsem,
            device_id=where, device_id_type=pl.DeviceIdType.MESH,
        )

    loads = [
        pltpu.make_async_copy(stiff.at[0], kx, load_sem.at[0]),
        pltpu.make_async_copy(mass.at[0], mx, load_sem.at[1]),
        pltpu.make_async_copy(vec, vx, load_sem.at[2]),
    ]
    for c in loads:
        c.start()

    def narrow_peer(d):
        return dev(z, xh, core, lax.rem(y + d // 2, 4) * 2 + lax.rem(xl + d % 2, 2))

    def x_at(xx):
        return dev(z, xx // 2, core, y * 2 + lax.rem(xx, 2))

    def y_at(yy):
        return dev(z, xh, core, yy * 2 + xl)

    sibling = dev(z, xh, 1 - core, n)
    zm4 = lax.rem(z, 4)
    is_mid = zm4 == 0
    owner = z // 8
    is_src = jnp.logical_and(lax.rem(z, 8) == 0, jnp.logical_and(xh == 0, core == 0))
    src_z = 8 * core

    def up(d):
        return dev(lax.rem(z + 16 + d, 16), xh, core, n)

    STEPS = (2, 1, -1)
    middle = dev(lax.rem(jnp.where(zm4 == 3, z + 1, z - zm4), 16), xh, core, n)

    barrier = pltpu.get_barrier_semaphore()

    def greet(where):
        pl.semaphore_signal(barrier, inc=1, device_id=where, device_id_type=pl.DeviceIdType.MESH)

    for d in range(1, 8):
        greet(narrow_peer(d))
    greet(x_at(lax.rem(x + 2, 4)))
    greet(x_at(lax.rem(jnp.where(xl == 0, x + 3, x + 1), 4)))
    greet(sibling)

    @pl.when(is_mid)
    def _():
        for d in STEPS:
            greet(up(d))

    @pl.when(jnp.logical_not(is_mid))
    def _():
        greet(middle)

    is_root = jnp.logical_and(z == src_z, xh == 1)
    feeds = jnp.logical_or(is_src, is_root)
    is_fed = jnp.logical_and(is_mid, z != src_z)
    crosses = jnp.logical_and(z == 8, core == xh)
    across = dev(z, 1 - xh, 1 - core, 2 * y + 1 - xl)

    def fed_plane(k):
        return dev(lax.rem(z + 4 * k, 16), xh, owner, n)

    @pl.when(feeds)
    def _():
        for k in range(1, 4):
            greet(fed_plane(k))

    @pl.when(is_fed)
    def _():
        greet(dev(src_z, xh, core * xh, n))

    @pl.when(crosses)
    def _():
        greet(across)

    pl.semaphore_wait(
        barrier,
        10
        + jnp.where(is_mid, 3, 1)
        + jnp.where(feeds, 3, 0)
        + jnp.where(is_fed, 1, 0)
        + jnp.where(crosses, 1, 0),
    )

    def a_rows(yy, xx):
        return pl.ds(yy * 16 + xx * 4, 4)

    def b_rows(yy, xx):
        return pl.ds(64 + xx * 16 + yy * 4, 4)

    mine_a = own.at[a_rows(y, x)]
    mine_b = own.at[b_rows(y, x)]

    def owner_copies(i):
        rows = (a_rows, b_rows)[i]
        first = pan_in.at[pl.ds(i * 4, 4)]
        second = pan_in.at[pl.ds(8 + i * 4, 4)]
        here = own.at[rows(y, xl)]
        there = own.at[rows(y, 3 - xl)]
        root = dev(z, 1, owner, 2 * y + 1 - xl)
        return (
            [remote(second, there, a_send.at[i, 0], a_recv.at[i], root)]
            + [remote(first, here, a_send.at[i, k], a_recv.at[i], fed_plane(k)) for k in (2, 1, 3)],
            pltpu.make_async_copy(first, here, a_recv.at[i]),
            remote(first, here, a_send.at[i, 4], a_recv.at[i], sibling),
        )

    @pl.when(is_src)
    def _():
        for i in range(2):
            far, local, near = owner_copies(i)
            for c in far:
                c.start()

            @pl.when(owner == 0)
            def _():
                local.start()

            @pl.when(owner == 1)
            def _():
                near.start()

    m = jnp.broadcast_to(imap[...], (8, ROWS))
    m = jnp.where(iota((8, ROWS), 0) == 0, lax.shift_right_logical(m, 7), jnp.bitwise_and(m, 127)).astype(F32).astype(BF16)
    lane = iota((128, 128), 1)
    row_of = (lane // 64) * 64 + jnp.bitwise_and(lane, 31) * 2 + jnp.bitwise_and(lane // 32, 1)
    swap = jnp.where(iota((128, 128), 0) == row_of, 1.0, 0.0).astype(BF16)
    tri = jnp.where(iota((128, 128), 0) < iota((128, 128), 1), 1.0, 0.0).astype(BF16)
    carry = jnp.zeros((8, 1), F32)
    idx_parts, spot_parts = [], []
    for b in range(8):
        t = jnp.dot(m[:, b * 128 : (b + 1) * 128], swap, preferred_element_type=F32).astype(jnp.int32)
        mb = t[0:1] * 128 + t[1:2]
        tb = lax.shift_right_logical(mb, 10)
        spot_parts.append(jnp.bitwise_and(mb, 1023) + 1)
        near = 2 * jnp.bitwise_and(lax.shift_right_logical(tb, 1) + 4 - y, 3) + jnp.bitwise_and(tb + xl, 1)
        hit = jnp.where(iota((8, 128), 0) == jnp.broadcast_to(tb, (8, 128)), 1.0, 0.0)
        before = jnp.dot(hit.astype(BF16), tri, preferred_element_type=F32) + carry
        carry = carry + jnp.sum(hit, axis=1, keepdims=True)
        rank = jnp.sum(hit * before, axis=0, keepdims=True)
        idx_parts.append(near * CAP + rank.astype(jnp.int32))
    idx = jnp.concatenate(idx_parts, axis=1)
    spot8 = jnp.broadcast_to(jnp.concatenate(spot_parts, axis=1), (8, ROWS))
    hi = lax.shift_right_logical(spot8, 5)
    lo = jnp.bitwise_and(spot8, 31)
    two = jnp.where(iota((8, ROWS), 0) == 0, hi, lo).astype(F32).astype(BF16)

    def build(g, _):
        rows = pl.ds(pl.multiple_of(g * CAP, CAP), CAP)
        s = jnp.where(iota((CAP, ROWS), 0) + g * CAP == idx, 1.0, 0.0).astype(BF16)
        sel[rows, :] = s
        t = lax.dot_general(two, s, (((1,), (1,)), ((), ())), preferred_element_type=F32)
        pos_s[g] = t
        return 0

    lax.fori_loop(0, 8, build, 0)

    pos_out = []
    for d in range(1, 8):
        c = remote(pos_s.at[d], pos_r.at[d], p_send.at[d], p_recv.at[d], narrow_peer(d))
        c.start()
        pos_out.append(c)
    pos_r[0] = pos_s[0]

    loads[2].wait()

    def flip(k, _):
        o = pl.ds(pl.multiple_of(k * 256, 256), 256)
        vt[:, o] = vx[o, :].T
        return 0

    lax.fori_loop(0, 4, flip, 0)
    f_out, b1_out, b1_in = [], [], []
    fed = (
        remote(mine_a, mine_a, a_send.at[0, 0], a_recv.at[0], sibling),
        remote(mine_b, mine_b, a_send.at[1, 0], a_recv.at[1], sibling),
    )
    for i, mine in enumerate((mine_a, mine_b)):
        fed[i].wait_recv()

        @pl.when(is_root)
        def _():
            for k in (2, 1, 3):
                remote(mine, mine, a_send.at[i, k], a_recv.at[i], fed_plane(k)).start()

        @pl.when(is_mid)
        def _():
            for k, d in enumerate(STEPS):
                remote(mine, mine, f_send.at[i, k], a_recv.at[i], up(d)).start()

        for d in (2, 1, 3):
            if i == 0:
                to, came = x_at(lax.rem(x + d, 4)), own.at[a_rows(y, lax.rem(x + 4 - d, 4))]
            else:
                to, came = y_at(lax.rem(y + d, 4)), own.at[b_rows(lax.rem(y + 4 - d, 4), x)]
            c = remote(mine, mine, b1_send.at[i, d], b1_recv.at[i, d], to)
            c.start()
            b1_out.append(c)
            b1_in.append(remote(came, came, b1_send.at[i, d], b1_recv.at[i, d], to))

    br = brow[...]
    bc = bcol[...]
    sq = (SLOTS, SLOTS)
    diag = iota(sq, 0) == iota(sq, 1)
    br_b = jnp.broadcast_to(br, sq)
    brc = jnp.sum(jnp.where(diag, br_b, 0), axis=1, keepdims=True)
    bcc = jnp.sum(jnp.where(diag, jnp.broadcast_to(bc, sq), 0), axis=1, keepdims=True)
    earlier = jnp.logical_and(iota(sq, 0) < iota(sq, 1), brc == br_b)
    rank = jnp.sum(jnp.where(earlier, 1, 0), axis=0, keepdims=True)
    same = iota((RB, SLOTS), 0) == jnp.broadcast_to(br, (RB, SLOTS))
    count = jnp.sum(jnp.where(same, 1, 0), axis=1, keepdims=True)
    padded = jnp.bitwise_and(count + 3, -4)
    off = jnp.sum(jnp.where(iota((RB, SLOTS), 0) < br, padded, 0), axis=0, keepdims=True)
    dest = jnp.where(br < RB, off + rank, 4096)
    destc = jnp.sum(jnp.where(diag, jnp.broadcast_to(dest, sq), 0), axis=1, keepdims=True)
    count_l = jnp.sum(jnp.where(brc == iota((SLOTS, 128), 1), 1, 0), axis=0, keepdims=True)
    padded_l = jnp.bitwise_and(count_l + 3, -4)
    off_c = jnp.sum(jnp.where(iota((RB, 128), 1) < iota((RB, 128), 0), padded_l, 0), axis=1, keepdims=True)
    begins = jnp.logical_and(lax.shift_right_logical(off_c, 2) == iota((RB, 256), 1), count > 0)
    keep = 1 - jnp.sum(jnp.where(begins, 1, 0), axis=0, keepdims=True)
    end_l = jnp.sum(jnp.where(iota((RB, 256), 0) <= iota((RB, 256), 1), padded, 0), axis=0, keepdims=True)
    last = jnp.maximum(lax.shift_right_logical(end_l, 2) - 1, 0)
    some = jnp.minimum(count_l, 1)
    some = jnp.concatenate([some, some], axis=1)
    q = jnp.bitwise_and(bcc, 3)
    part = jnp.bitwise_and(lax.shift_right_logical(bcc, 2), 1)
    bxl = jnp.bitwise_and(lax.shift_right_logical(bcc, 4), 1)
    bx = jnp.where(jnp.bitwise_and(bcc, 8) == 8, 3 - bxl, bxl)
    by = lax.shift_right_logical(bcc, 5)
    place = jnp.where(part == 1, 64 + bx * 16 + by * 4, by * 16 + bx * 4) + q
    block = jnp.sum(jnp.where(destc == iota((SLOTS, 256), 1), place, 0), axis=0, keepdims=True)
    r8 = iota((8, 256), 0)
    meta[...] = jnp.where(r8 == 0, block, jnp.where(r8 == 1, keep, jnp.where(r8 == 2, last, some)))
    to_scalar = pltpu.make_async_copy(meta, meta_s, meta_sem)
    to_scalar.start()
    perm[...] = jnp.where(iota((SORTED, SLOTS), 0) == dest, 1.0, 0.0).astype(BF16)

    loads[0].wait()
    loads[1].wait()

    def order(j, _):
        lanes = pl.ds(pl.multiple_of(j * 512, 512), 512)
        for src, dst in ((kx, zk), (mx, zm)):
            t = jnp.dot(perm[...], src[:, lanes], preferred_element_type=F32)
            for i in range(4):
                dst[pl.ds(j * 4 + i, SORTED, stride=32), :] = t[:, i * 128 : (i + 1) * 128]
        return 0

    lax.fori_loop(0, 8, order, 0)
    row_a = own.at[pl.ds(y * 16, 16)]
    row_b = own.at[pl.ds(64 + x * 16, 16)]
    far_a = other.at[pl.ds(y * 16, 16)]
    far_b = other.at[pl.ds(64 + x * 16, 16)]
    b2_out, b2_in, c_out = [], [], []
    for i in range(2):
        block_ref = (row_a, row_b)[i]
        for c in b1_in[i * 3 : i * 3 + 3]:
            c.wait_recv()
        for d in (2, 1, 3):
            if i == 0:
                to, o = y_at(lax.rem(y + d, 4)), lax.rem(y + 4 - d, 4) * 16
            else:
                to, o = x_at(lax.rem(x + d, 4)), 64 + lax.rem(x + 4 - d, 4) * 16
            c = remote(block_ref, block_ref, b2_send.at[i, d], b2_recv.at[i, d], to)
            c.start()
            b2_out.append(c)
            came = own.at[pl.ds(o, 16)]
            b2_in.append((came, o, d, remote(came, came, b2_send.at[i, d], b2_recv.at[i, d], to)))
        c = remote(block_ref, (far_a, far_b)[i], c_send.at[i], c_recv.at[i], sibling)
        c.start()
        c_out.append(c)

    left = iota((32, 128), 1) < 64

    def assemble(g, _):
        for mat, src in enumerate((zk, zm)):
            for pair in range(2):
                o = pl.multiple_of(g * 128 + pair * 64, 64)
                t0 = src[pl.ds(o, 32), :]
                t1 = src[pl.ds(o + 32, 32), :]
                even = jnp.where(left, t0, pltpu.roll(t1, 64, 1))
                odd = jnp.where(left, pltpu.roll(t0, 64, 1), t1)
                lhs[g, mat * 64 : mat * 64 + 32, pair * 128 : (pair + 1) * 128] = even.astype(BF16)
                lhs[g, mat * 64 + 32 : mat * 64 + 64, pair * 128 : (pair + 1) * 128] = odd.astype(BF16)
        return 0

    def assemble4(g4, _):
        for u in range(4):
            assemble(g4 * 4 + u, 0)
        return 0

    lax.fori_loop(0, GROUPS // 4, assemble4, 0)

    for d in range(1, 8):
        pos_out[d - 1].wait_recv()

    def weigh(d, _):
        t = pos_r[d]
        at = (t[0:1, :] * 32.0 + t[1:2, :]).astype(jnp.int32)
        q_d = jnp.where(iota((ROWS, CAP), 0) + 1 == at, 1.0, 0.0).astype(BF16)
        wts[:, pl.ds(pl.multiple_of(d * CAP, CAP), CAP)] = jnp.dot(
            vt[...], q_d, preferred_element_type=F32
        ).astype(BF16)
        return 0

    lax.fori_loop(0, 8, weigh, 0)

    for k, (came, o, d, c) in enumerate(b2_in):
        c.wait_recv()
        h = remote(came, other.at[pl.ds(o, 16)], c_send.at[2 + k], c_recv.at[2 + k], sibling)
        h.start()
        c_out.append(h)
    to_scalar.wait()

    x_out = []
    for half in range(2):
        pan = (own, other)[half]
        if half == 1:
            offs = [y * 16, 64 + x * 16] + [o for _, o, _, _ in b2_in]
            for k, o in enumerate(offs):
                came = other.at[pl.ds(o, 16)]
                remote(came, came, c_send.at[k], c_recv.at[k], sibling).wait_recv()

        def multiply(g4, held):
            for u in range(4):
                g = g4 * 4 + u
                rhs = jnp.concatenate([pan[meta_s[0, g * 4 + i]] for i in range(4)], axis=0)
                t = jnp.dot(lhs[g], rhs, preferred_element_type=F32)
                held = t + held * meta_s[1, g].astype(F32)
                run[g] = held
            return held

        lax.fori_loop(0, GROUPS // 4, multiply, jnp.zeros((128, PC), F32))

        def collect(r, _):
            t = run[meta_s[2, r]] * meta_s[3, r].astype(F32)
            rows = pl.ds(pl.multiple_of(r * BLK, BLK), BLK)
            prod[rows, 0:PC] = t[0:BLK].astype(BF16)
            prod[rows, PC : 2 * PC] = t[BLK : 2 * BLK].astype(BF16)
            return 0

        lax.fori_loop(0, RB, collect, 0)

        for first in (4, 0):
            rows = pl.ds(first * CAP, 4 * CAP)
            t = jnp.dot(sel[rows, :], prod[...], preferred_element_type=F32).astype(BF16)
            for d in range(first, first + 4):
                td = t[(d - first) * CAP : (d - first + 1) * CAP]
                if d == 0:
                    recv[half, 0:CAP, :] = td
                else:
                    send[half, d] = td
                    c = remote(
                        send.at[half, d], recv.at[half, d * CAP : (d + 1) * CAP],
                        x_send.at[half, d], x_recv.at[half, d], narrow_peer(d),
                    )
                    c.start()
                    x_out.append(c)

    for half in range(2):
        which = core if half == 0 else 1 - core
        for c in x_out[half * 7 : half * 7 + 7]:
            c.wait_recv()
        t = jnp.dot(wts[...], recv[half], preferred_element_type=F32)
        out[:, pl.ds(pl.multiple_of(which * 2 * PC, 2 * PC), 2 * PC)] = t.astype(BF16)

    for c in pos_out + b1_out + b2_out + c_out + x_out:
        c.wait_send()

    @pl.when(is_mid)
    def _():
        for i, mine in enumerate((mine_a, mine_b)):
            for k, d in enumerate(STEPS):
                remote(mine, mine, f_send.at[i, k], a_recv.at[i], up(d)).wait_send()

    @pl.when(is_root)
    def _():
        for i, mine in enumerate((mine_a, mine_b)):
            for k in (2, 1, 3):
                remote(mine, mine, a_send.at[i, k], a_recv.at[i], fed_plane(k)).wait_send()

    @pl.when(is_src)
    def _():
        for i in range(2):
            far, local, near = owner_copies(i)
            for c in far:
                c.wait_send()

            @pl.when(owner == 1)
            def _():
                near.wait_send()


def body(panels, stiff_blocks, mass_blocks, block_rows, block_cols, interface_map, cond_vectors):
    hbm = pl.BlockSpec(memory_space=pl.ANY)
    vmem = pl.BlockSpec(memory_space=pltpu.VMEM)
    dma = pltpu.SemaphoreType.DMA
    res = pl.pallas_call(
        kernel,
        out_shape=jax.ShapeDtypeStruct((NC, 4 * PC), BF16),
        in_specs=[hbm, hbm, hbm, vmem, vmem, vmem, hbm],
        out_specs=vmem,
        scratch_shapes=[
            pltpu.VMEM((128, BLK, PC), BF16),
            pltpu.VMEM((128, BLK, PC), BF16),
            pltpu.VMEM((SLOTS, BLK * BLK), BF16),
            pltpu.VMEM((SLOTS, BLK * BLK), BF16),
            pltpu.VMEM((ROWS, NC), BF16),
            pltpu.VMEM((NC, ROWS), BF16),
            pltpu.VMEM((SORTED, SLOTS), BF16),
            pltpu.VMEM((SORTED * 32, 128), F32),
            pltpu.VMEM((SORTED * 32, 128), F32),
            pltpu.VMEM((GROUPS, 128, 256), BF16),
            pltpu.VMEM((GROUPS, 128, PC), F32),
            pltpu.VMEM((ROWS, 2 * PC), BF16),
            pltpu.VMEM((8 * CAP, ROWS), BF16),
            pltpu.VMEM((NC, 8 * CAP), BF16),
            pltpu.VMEM((8, 8, CAP), F32),
            pltpu.VMEM((8, 8, CAP), F32),
            pltpu.VMEM((2, 8, CAP, 2 * PC), BF16),
            pltpu.VMEM((2, 8 * CAP, 2 * PC), BF16),
            pltpu.VMEM((8, 256), jnp.int32),
            pltpu.SMEM((8, 256), jnp.int32),
            dma((3,)), dma, dma((2, 8)), dma((2,)), dma((2, 3)), dma((2, 4)), dma((2, 4)), dma((2, 4)), dma((2, 4)),
            dma((8,)), dma((8,)), dma((8,)), dma((8,)), dma((2, 8)), dma((2, 8)),
        ],
        compiler_params=pltpu.CompilerParams(
            collective_id=0, has_side_effects=True, vmem_limit_bytes=60 * 2**20
        ),
    )(panels.reshape(RB, BLK, PC), stiff_blocks, mass_blocks, block_rows, block_cols, interface_map, cond_vectors)
    return res.reshape(1, 1, NC, 4 * PC)


def solution(mesh):
    return jax.shard_map(
        body,
        mesh=mesh,
        in_specs=(
            P("wide", "narrow", None),
            P("wide", "narrow", None),
            P("wide", "narrow", None),
            P("wide", "narrow"),
            P("wide", "narrow"),
            P("wide", "narrow"),
            P("narrow", None),
        ),
        out_specs=P("wide", "narrow", None, None),
        check_vma=False,
    )
```

```python
import jax
import jax.numpy as jnp
from jax import lax
from jax.experimental import pallas as pl
from jax.experimental.pallas import tpu as pltpu
from jax.sharding import PartitionSpec as P

BLK = 64
PC = 128
NC = 768
RB = 16
SLOTS = 152
ROWS = 1024
CAP = 256
GROUPS = 52
SORTED = GROUPS * 4
F32 = jnp.float32
BF16 = jnp.bfloat16


def iota(shape, dim):
    return lax.broadcasted_iota(jnp.int32, shape, dim)


def kernel(
    pan_in, stiff, mass, brow, bcol, imap, vec, out,
    pan_0, pan_1, kx, mx, vx, vt, perm, zk, zm, lhs, run, prod, sel, wts, pos_s, pos_r, send, recv,
    meta, meta_s,
    load_sem, meta_sem, a_send, a_recv, f_send, b1_send, b1_recv, b2_send, b2_recv,
    c_send, c_recv, p_send, p_recv, x_send, x_recv,
):
    w = lax.axis_index("wide")
    n = lax.axis_index("narrow")
    core = lax.rem(w, 2)
    xh = lax.rem(w // 2, 2)
    z = w // 4
    y = n // 2
    xl = lax.rem(n, 2)
    x = 2 * xh + xl

    def dev(z_, xh_, core_, n_):
        return {"wide": z_ * 4 + xh_ * 2 + core_, "narrow": n_}

    def remote(src, dst, ssem, rsem, where):
        return pltpu.make_async_remote_copy(
            src_ref=src, dst_ref=dst, send_sem=ssem, recv_sem=rsem,
            device_id=where, device_id_type=pl.DeviceIdType.MESH,
        )

    loads = [
        pltpu.make_async_copy(stiff.at[0], kx, load_sem.at[0]),
        pltpu.make_async_copy(mass.at[0], mx, load_sem.at[1]),
        pltpu.make_async_copy(vec, vx, load_sem.at[2]),
    ]
    for c in loads:
        c.start()

    def narrow_peer(d):
        return dev(z, xh, core, lax.rem(y + d // 2, 4) * 2 + lax.rem(xl + d % 2, 2))

    def x_at(xx):
        return dev(z, xx // 2, core, y * 2 + lax.rem(xx, 2))

    def y_at(yy):
        return dev(z, xh, core, yy * 2 + xl)

    sibling = dev(z, xh, 1 - core, n)
    zm4 = lax.rem(z, 4)
    is_mid = zm4 == 0
    owner = z // 8
    at_owner = lax.rem(z, 8) == 0
    is_src = jnp.logical_and(at_owner, jnp.logical_and(xh == 0, core == 0))
    is_root = jnp.logical_and(at_owner, xh == 1)
    crosses = jnp.logical_and(is_root, core == 1)
    pans = (pan_0, pan_1)

    def up(d):
        return dev(lax.rem(z + 16 + d, 16), xh, core, n)

    STEPS = (2, 1, -1)
    middle = dev(lax.rem(jnp.where(zm4 == 3, z + 1, z - zm4), 16), xh, core, n)

    def fed_plane(k, core_):
        return dev(lax.rem(z + 4 * k, 16), xh, core_, n)

    across = 2 * y + 1 - xl

    barrier = pltpu.get_barrier_semaphore()

    def greet(where):
        pl.semaphore_signal(barrier, inc=1, device_id=where, device_id_type=pl.DeviceIdType.MESH)

    for d in range(1, 8):
        greet(narrow_peer(d))
    greet(x_at(lax.rem(x + 2, 4)))
    greet(x_at(lax.rem(jnp.where(xl == 0, x + 3, x + 1), 4)))
    greet(sibling)

    @pl.when(is_mid)
    def _():
        for d in STEPS:
            greet(up(d))

    @pl.when(jnp.logical_not(is_mid))
    def _():
        greet(middle)

    @pl.when(is_src)
    def _():
        for k in range(1, 4):
            greet(fed_plane(k, 0))
            greet(fed_plane(k, 1))
        greet(dev(z, 1, 1, across))

    @pl.when(is_root)
    def _():
        for k in range(1, 4):
            greet(fed_plane(k, core))

    @pl.when(crosses)
    def _():
        greet(dev(z, 0, 0, across))

    for p in range(2):
        @pl.when(jnp.logical_and(is_mid, z != 8 * p))
        def _():
            greet(dev(8 * p, xh, core * xh, n))

    pl.semaphore_wait(
        barrier,
        10
        + jnp.where(is_mid, 3, 1)
        + jnp.where(is_src, 7, 0)
        + jnp.where(is_root, 3, 0)
        + jnp.where(crosses, 1, 0)
        + jnp.where(jnp.logical_and(is_mid, z != 0), 1, 0)
        + jnp.where(jnp.logical_and(is_mid, z != 8), 1, 0),
    )

    def spot_of(core_, yy, xx):
        return jnp.where(core_ == 0, yy * 16 + xx * 4, 64 + xx * 16 + yy * 4)

    mine_at = spot_of(core, y, x)
    line_at = jnp.where(core == 0, y * 16, 64 + x * 16)

    def owner_copies(p):
        far, near = [], []
        for c in range(2):
            first = pan_in.at[pl.ds(c * 4, 4)]
            second = pan_in.at[pl.ds(8 + c * 4, 4)]
            here = pans[p].at[pl.ds(64 * c + (y * 16 + xl * 4 if c == 0 else xl * 16 + y * 4), 4)]
            there = pans[p].at[pl.ds(64 * c + (y * 16 + (3 - xl) * 4 if c == 0 else (3 - xl) * 16 + y * 4), 4)]
            far.append(remote(second, there, a_send.at[c, 0], a_recv.at[p], dev(z, 1, c, across)))
            for k in (2, 1, 3):
                far.append(remote(first, here, a_send.at[c, k], a_recv.at[p], fed_plane(k, c)))
            if c == 0:
                near.append(pltpu.make_async_copy(first, here, a_recv.at[p]))
            else:
                far.append(remote(first, here, a_send.at[c, 4], a_recv.at[p], sibling))
        return far, near

    for p in range(2):
        @pl.when(jnp.logical_and(is_src, owner == p))
        def _():
            far, near = owner_copies(p)
            for c in near + far:
                c.start()

    def first_round(p, d):
        mine = pans[p].at[pl.ds(mine_at, 4)]
        xx, yy = lax.rem(x + 4 - d, 4), lax.rem(y + 4 - d, 4)
        came = pans[p].at[pl.ds(jnp.where(core == 0, y * 16 + xx * 4, 64 + x * 16 + yy * 4), 4)]
        to_x = lax.rem(x + d, 4)
        to_w = z * 4 + jnp.where(core == 0, to_x // 2, xh) * 2 + core
        to_n = jnp.where(core == 0, y * 2 + lax.rem(to_x, 2), lax.rem(y + d, 4) * 2 + xl)
        sems = b1_send.at[p, d], b1_recv.at[p, d], {"wide": to_w, "narrow": to_n}
        return remote(mine, mine, *sems), remote(came, came, *sems)

    def second_round(p, d):
        line = pans[p].at[pl.ds(line_at, 16)]
        o = jnp.where(core == 0, lax.rem(y + 4 - d, 4) * 16, 64 + lax.rem(x + 4 - d, 4) * 16)
        came = pans[p].at[pl.ds(o, 16)]
        to_x = lax.rem(x + d, 4)
        to_w = z * 4 + jnp.where(core == 1, to_x // 2, xh) * 2 + core
        to_n = jnp.where(core == 1, y * 2 + lax.rem(to_x, 2), lax.rem(y + d, 4) * 2 + xl)
        sems = b2_send.at[p, d], b2_recv.at[p, d], {"wide": to_w, "narrow": to_n}
        return remote(line, line, *sems), remote(came, came, *sems)

    def to_sibling(p, d):
        a, b = lax.rem(y + 4 - d, 4) * 16, 64 + lax.rem(x + 4 - d, 4) * 16
        gone = pans[p].at[pl.ds(jnp.where(core == 0, a, b), 16)]
        came = pans[p].at[pl.ds(jnp.where(core == 0, b, a), 16)]
        sems = c_send.at[p, d], c_recv.at[p, d], sibling
        return remote(gone, gone, *sems), remote(came, came, *sems)

    def pass_on(p):
        mine = pans[p].at[pl.ds(mine_at, 4)]
        remote(mine, mine, a_send.at[0, 0], a_recv.at[p], sibling).wait_recv()

        @pl.when(jnp.logical_and(is_root, owner == p))
        def _():
            for k in (2, 1, 3):
                remote(mine, mine, a_send.at[0, k], a_recv.at[p], fed_plane(k, core)).start()

        @pl.when(is_mid)
        def _():
            for k, d in enumerate(STEPS):
                remote(mine, mine, f_send.at[p, k], a_recv.at[p], up(d)).start()

        for d in (2, 1, 3):
            first_round(p, d)[0].start()

    @pl.when(jnp.logical_and(is_mid, z == 8))
    def _():
        pass_on(1)
        pass_on(0)

    @pl.when(jnp.logical_and(is_mid, z != 8))
    def _():
        pass_on(0)
        pass_on(1)

    m = jnp.broadcast_to(imap[...], (8, ROWS))
    m = jnp.where(iota((8, ROWS), 0) == 0, lax.shift_right_logical(m, 7), jnp.bitwise_and(m, 127)).astype(F32).astype(BF16)
    lane = iota((128, 128), 1)
    row_of = (lane // 64) * 64 + jnp.bitwise_and(lane, 31) * 2 + jnp.bitwise_and(lane // 32, 1)
    swap = jnp.where(iota((128, 128), 0) == row_of, 1.0, 0.0).astype(BF16)
    tri = jnp.where(iota((128, 128), 0) < iota((128, 128), 1), 1.0, 0.0).astype(BF16)
    carry = jnp.zeros((8, 1), F32)
    idx_parts, spot_parts = [], []
    for b in range(8):
        t = jnp.dot(m[:, b * 128 : (b + 1) * 128], swap, preferred_element_type=F32).astype(jnp.int32)
        mb = t[0:1] * 128 + t[1:2]
        tb = lax.shift_right_logical(mb, 10)
        spot_parts.append(jnp.bitwise_and(mb, 1023) + 1)
        near = 2 * jnp.bitwise_and(lax.shift_right_logical(tb, 1) + 4 - y, 3) + jnp.bitwise_and(tb + xl, 1)
        hit = jnp.where(iota((8, 128), 0) == jnp.broadcast_to(tb, (8, 128)), 1.0, 0.0)
        before = jnp.dot(hit.astype(BF16), tri, preferred_element_type=F32) + carry
        carry = carry + jnp.sum(hit, axis=1, keepdims=True)
        rank = jnp.sum(hit * before, axis=0, keepdims=True)
        idx_parts.append(near * CAP + rank.astype(jnp.int32))
    idx = jnp.concatenate(idx_parts, axis=1)
    spot8 = jnp.broadcast_to(jnp.concatenate(spot_parts, axis=1), (8, ROWS))
    hi = lax.shift_right_logical(spot8, 5)
    lo = jnp.bitwise_and(spot8, 31)
    two = jnp.where(iota((8, ROWS), 0) == 0, hi, lo).astype(F32).astype(BF16)

    def build(g, _):
        rows = pl.ds(pl.multiple_of(g * CAP, CAP), CAP)
        s = jnp.where(iota((CAP, ROWS), 0) + g * CAP == idx, 1.0, 0.0).astype(BF16)
        sel[rows, :] = s
        t = lax.dot_general(two, s, (((1,), (1,)), ((), ())), preferred_element_type=F32)
        pos_s[g] = t
        return 0

    lax.fori_loop(0, 8, build, 0)

    pos_out = []
    for d in range(1, 8):
        c = remote(pos_s.at[d], pos_r.at[d], p_send.at[d], p_recv.at[d], narrow_peer(d))
        c.start()
        pos_out.append(c)
    pos_r[0] = pos_s[0]

    loads[2].wait()

    def flip(k, _):
        o = pl.ds(pl.multiple_of(k * 256, 256), 256)
        vt[:, o] = vx[o, :].T
        return 0

    lax.fori_loop(0, 4, flip, 0)
    br = brow[...]
    bc = bcol[...]
    sq = (SLOTS, SLOTS)
    diag = iota(sq, 0) == iota(sq, 1)
    br_b = jnp.broadcast_to(br, sq)
    brc = jnp.sum(jnp.where(diag, br_b, 0), axis=1, keepdims=True)
    bcc = jnp.sum(jnp.where(diag, jnp.broadcast_to(bc, sq), 0), axis=1, keepdims=True)
    earlier = jnp.logical_and(iota(sq, 0) < iota(sq, 1), brc == br_b)
    rank = jnp.sum(jnp.where(earlier, 1, 0), axis=0, keepdims=True)
    same = iota((RB, SLOTS), 0) == jnp.broadcast_to(br, (RB, SLOTS))
    count = jnp.sum(jnp.where(same, 1, 0), axis=1, keepdims=True)
    padded = jnp.bitwise_and(count + 3, -4)
    off = jnp.sum(jnp.where(iota((RB, SLOTS), 0) < br, padded, 0), axis=0, keepdims=True)
    dest = jnp.where(br < RB, off + rank, 4096)
    destc = jnp.sum(jnp.where(diag, jnp.broadcast_to(dest, sq), 0), axis=1, keepdims=True)
    count_l = jnp.sum(jnp.where(brc == iota((SLOTS, 128), 1), 1, 0), axis=0, keepdims=True)
    padded_l = jnp.bitwise_and(count_l + 3, -4)
    off_c = jnp.sum(jnp.where(iota((RB, 128), 1) < iota((RB, 128), 0), padded_l, 0), axis=1, keepdims=True)
    begins = jnp.logical_and(lax.shift_right_logical(off_c, 2) == iota((RB, 256), 1), count > 0)
    keep = 1 - jnp.sum(jnp.where(begins, 1, 0), axis=0, keepdims=True)
    end_l = jnp.sum(jnp.where(iota((RB, 256), 0) <= iota((RB, 256), 1), padded, 0), axis=0, keepdims=True)
    last = jnp.maximum(lax.shift_right_logical(end_l, 2) - 1, 0)
    some = jnp.minimum(count_l, 1)
    some = jnp.concatenate([some, some], axis=1)
    q = jnp.bitwise_and(bcc, 3)
    part = jnp.bitwise_and(lax.shift_right_logical(bcc, 2), 1)
    bxl = jnp.bitwise_and(lax.shift_right_logical(bcc, 4), 1)
    bx = jnp.where(jnp.bitwise_and(bcc, 8) == 8, 3 - bxl, bxl)
    by = lax.shift_right_logical(bcc, 5)
    place = jnp.where(part == 1, 64 + bx * 16 + by * 4, by * 16 + bx * 4) + q
    block = jnp.sum(jnp.where(destc == iota((SLOTS, 256), 1), place, 0), axis=0, keepdims=True)
    r8 = iota((8, 256), 0)
    meta[...] = jnp.where(r8 == 0, block, jnp.where(r8 == 1, keep, jnp.where(r8 == 2, last, some)))
    to_scalar = pltpu.make_async_copy(meta, meta_s, meta_sem)
    to_scalar.start()
    perm[...] = jnp.where(iota((SORTED, SLOTS), 0) == dest, 1.0, 0.0).astype(BF16)

    loads[0].wait()
    loads[1].wait()

    def order(j, _):
        lanes = pl.ds(pl.multiple_of(j * 512, 512), 512)
        for src, dst in ((kx, zk), (mx, zm)):
            t = jnp.dot(perm[...], src[:, lanes], preferred_element_type=F32)
            for i in range(4):
                dst[pl.ds(j * 4 + i, SORTED, stride=32), :] = t[:, i * 128 : (i + 1) * 128]
        return 0

    lax.fori_loop(0, 8, order, 0)
    @pl.when(jnp.logical_not(is_mid))
    def _():
        pass_on(0)
        pass_on(1)

    def begin_second(p):
        for d in (2, 1, 3):
            first_round(p, d)[1].wait_recv()
        for d in (2, 1, 3):
            second_round(p, d)[0].start()
        to_sibling(p, 0)[0].start()

    def hand_over(p):
        for d in (2, 1, 3):
            second_round(p, d)[1].wait_recv()
            to_sibling(p, d)[0].start()

    begin_second(0)
    left = iota((32, 128), 1) < 64

    def assemble(g, _):
        for mat, src in enumerate((zk, zm)):
            for pair in range(2):
                o = pl.multiple_of(g * 128 + pair * 64, 64)
                t0 = src[pl.ds(o, 32), :]
                t1 = src[pl.ds(o + 32, 32), :]
                even = jnp.where(left, t0, pltpu.roll(t1, 64, 1))
                odd = jnp.where(left, pltpu.roll(t0, 64, 1), t1)
                lhs[g, mat * 64 : mat * 64 + 32, pair * 128 : (pair + 1) * 128] = even.astype(BF16)
                lhs[g, mat * 64 + 32 : mat * 64 + 64, pair * 128 : (pair + 1) * 128] = odd.astype(BF16)
        return 0

    def assemble4(g4, _):
        for u in range(4):
            assemble(g4 * 4 + u, 0)
        return 0

    lax.fori_loop(0, GROUPS // 4, assemble4, 0)

    hand_over(0)
    begin_second(1)
    to_scalar.wait()

    x_out = []
    for half in range(2):
        pan = pans[half]
        if half == 1:
            hand_over(1)
        for d in (0, 2, 1, 3):
            to_sibling(half, d)[1].wait_recv()

        def multiply(g4, held):
            for u in range(4):
                g = g4 * 4 + u
                rhs = jnp.concatenate([pan[meta_s[0, g * 4 + i]] for i in range(4)], axis=0)
                t = jnp.dot(lhs[g], rhs, preferred_element_type=F32)
                held = t + held * meta_s[1, g].astype(F32)
                run[g] = held
            return held

        lax.fori_loop(0, GROUPS // 4, multiply, jnp.zeros((128, PC), F32))

        def collect(r, _):
            t = run[meta_s[2, r]] * meta_s[3, r].astype(F32)
            rows = pl.ds(pl.multiple_of(r * BLK, BLK), BLK)
            prod[rows, 0:PC] = t[0:BLK].astype(BF16)
            prod[rows, PC : 2 * PC] = t[BLK : 2 * BLK].astype(BF16)
            return 0

        lax.fori_loop(0, RB, collect, 0)

        for first in (4, 0):
            rows = pl.ds(first * CAP, 4 * CAP)
            t = jnp.dot(sel[rows, :], prod[...], preferred_element_type=F32).astype(BF16)
            for d in range(first, first + 4):
                td = t[(d - first) * CAP : (d - first + 1) * CAP]
                if d == 0:
                    recv[half, 0:CAP, :] = td
                else:
                    send[half, d] = td
                    c = remote(
                        send.at[half, d], recv.at[half, d * CAP : (d + 1) * CAP],
                        x_send.at[half, d], x_recv.at[half, d], narrow_peer(d),
                    )
                    c.start()
                    x_out.append(c)

    for d in range(1, 8):
        pos_out[d - 1].wait_recv()

    def weigh(d, _):
        t = pos_r[d]
        at = (t[0:1, :] * 32.0 + t[1:2, :]).astype(jnp.int32)
        q_d = jnp.where(iota((ROWS, CAP), 0) + 1 == at, 1.0, 0.0).astype(BF16)
        wts[:, pl.ds(pl.multiple_of(d * CAP, CAP), CAP)] = jnp.dot(
            vt[...], q_d, preferred_element_type=F32
        ).astype(BF16)
        return 0

    lax.fori_loop(0, 8, weigh, 0)

    for half in range(2):
        for c in x_out[half * 7 : half * 7 + 7]:
            c.wait_recv()
        t = jnp.dot(wts[...], recv[half], preferred_element_type=F32)
        out[:, half * 2 * PC : (half + 1) * 2 * PC] = t.astype(BF16)

    for p in range(2):
        for d in (2, 1, 3):
            first_round(p, d)[0].wait_send()
            second_round(p, d)[0].wait_send()
        for d in range(4):
            to_sibling(p, d)[0].wait_send()
    for c in pos_out + x_out:
        c.wait_send()

    for p in range(2):
        mine = pans[p].at[pl.ds(mine_at, 4)]

        @pl.when(is_mid)
        def _():
            for k, d in enumerate(STEPS):
                remote(mine, mine, f_send.at[p, k], a_recv.at[p], up(d)).wait_send()

        @pl.when(jnp.logical_and(is_root, owner == p))
        def _():
            for k in (2, 1, 3):
                remote(mine, mine, a_send.at[0, k], a_recv.at[p], fed_plane(k, core)).wait_send()

        @pl.when(jnp.logical_and(is_src, owner == p))
        def _():
            for c in owner_copies(p)[0]:
                c.wait_send()


def body(panels, stiff_blocks, mass_blocks, block_rows, block_cols, interface_map, cond_vectors):
    hbm = pl.BlockSpec(memory_space=pl.ANY)
    vmem = pl.BlockSpec(memory_space=pltpu.VMEM)
    dma = pltpu.SemaphoreType.DMA
    res = pl.pallas_call(
        kernel,
        out_shape=jax.ShapeDtypeStruct((NC, 4 * PC), BF16),
        in_specs=[hbm, hbm, hbm, vmem, vmem, vmem, hbm],
        out_specs=vmem,
        scratch_shapes=[
            pltpu.VMEM((128, BLK, PC), BF16),
            pltpu.VMEM((128, BLK, PC), BF16),
            pltpu.VMEM((SLOTS, BLK * BLK), BF16),
            pltpu.VMEM((SLOTS, BLK * BLK), BF16),
            pltpu.VMEM((ROWS, NC), BF16),
            pltpu.VMEM((NC, ROWS), BF16),
            pltpu.VMEM((SORTED, SLOTS), BF16),
            pltpu.VMEM((SORTED * 32, 128), F32),
            pltpu.VMEM((SORTED * 32, 128), F32),
            pltpu.VMEM((GROUPS, 128, 256), BF16),
            pltpu.VMEM((GROUPS, 128, PC), F32),
            pltpu.VMEM((ROWS, 2 * PC), BF16),
            pltpu.VMEM((8 * CAP, ROWS), BF16),
            pltpu.VMEM((NC, 8 * CAP), BF16),
            pltpu.VMEM((8, 8, CAP), F32),
            pltpu.VMEM((8, 8, CAP), F32),
            pltpu.VMEM((2, 8, CAP, 2 * PC), BF16),
            pltpu.VMEM((2, 8 * CAP, 2 * PC), BF16),
            pltpu.VMEM((8, 256), jnp.int32),
            pltpu.SMEM((8, 256), jnp.int32),
            dma((3,)), dma, dma((2, 8)), dma((2,)), dma((2, 3)), dma((2, 4)), dma((2, 4)), dma((2, 4)), dma((2, 4)),
            dma((2, 4)), dma((2, 4)), dma((8,)), dma((8,)), dma((2, 8)), dma((2, 8)),
        ],
        compiler_params=pltpu.CompilerParams(
            collective_id=0, has_side_effects=True, vmem_limit_bytes=60 * 2**20
        ),
    )(panels.reshape(RB, BLK, PC), stiff_blocks, mass_blocks, block_rows, block_cols, interface_map, cond_vectors)
    return res.reshape(1, 1, NC, 4 * PC)


def solution(mesh):
    return jax.shard_map(
        body,
        mesh=mesh,
        in_specs=(
            P("wide", "narrow", None),
            P("wide", "narrow", None),
            P("wide", "narrow", None),
            P("wide", "narrow"),
            P("wide", "narrow"),
            P("wide", "narrow"),
            P("narrow", None),
        ),
        out_specs=P("wide", "narrow", None, None),
        check_vma=False,
    )
```

```python
import jax
import jax.numpy as jnp
from jax import lax
from jax.experimental import pallas as pl
from jax.experimental.pallas import tpu as pltpu
from jax.sharding import PartitionSpec as P

BLK = 64
PC = 128
NC = 768
RB = 16
SLOTS = 152
ROWS = 1024
CAP = 256
GROUPS = 52
SORTED = GROUPS * 4
F32 = jnp.float32
BF16 = jnp.bfloat16


def iota(shape, dim):
    return lax.broadcasted_iota(jnp.int32, shape, dim)


def kernel(
    pan_in, stiff, mass, brow, bcol, imap, vec, out,
    own, other, kx, mx, vx, vt, perm, zk, zm, lhs, run, prod, sel, wts, pos_s, pos_r, send, recv,
    meta, meta_s,
    load_sem, meta_sem, a_send, a_recv, f_send, b1_send, b1_recv, b2_send, b2_recv,
    c_send, c_recv, p_send, p_recv, x_send, x_recv,
):
    w = lax.axis_index("wide")
    n = lax.axis_index("narrow")
    core = lax.rem(w, 2)
    xh = lax.rem(w // 2, 2)
    z = w // 4
    y = n // 2
    xl = lax.rem(n, 2)
    x = 2 * xh + xl

    def dev(z_, xh_, core_, n_):
        return {"wide": z_ * 4 + xh_ * 2 + core_, "narrow": n_}

    def remote(src, dst, ssem, rsem, where):
        return pltpu.make_async_remote_copy(
            src_ref=src, dst_ref=dst, send_sem=ssem, recv_sem=rsem,
            device_id=where, device_id_type=pl.DeviceIdType.MESH,
        )

    loads = [
        pltpu.make_async_copy(stiff.at[0], kx, load_sem.at[0]),
        pltpu.make_async_copy(mass.at[0], mx, load_sem.at[1]),
        pltpu.make_async_copy(vec, vx, load_sem.at[2]),
    ]
    for c in loads:
        c.start()

    def narrow_peer(d):
        return dev(z, xh, core, lax.rem(y + d // 2, 4) * 2 + lax.rem(xl + d % 2, 2))

    def x_at(xx):
        return dev(z, xx // 2, core, y * 2 + lax.rem(xx, 2))

    def y_at(yy):
        return dev(z, xh, core, yy * 2 + xl)

    sibling = dev(z, xh, 1 - core, n)
    zm4 = lax.rem(z, 4)
    is_mid = zm4 == 0
    owner = z // 8
    is_src = jnp.logical_and(lax.rem(z, 8) == 0, jnp.logical_and(xh == 0, core == 0))
    src_z = 8 * core

    def up(d):
        return dev(lax.rem(z + 16 + d, 16), xh, core, n)

    STEPS = (2, 1, -1)
    middle = dev(lax.rem(jnp.where(zm4 == 3, z + 1, z - zm4), 16), xh, core, n)

    barrier = pltpu.get_barrier_semaphore()

    def greet(where):
        pl.semaphore_signal(barrier, inc=1, device_id=where, device_id_type=pl.DeviceIdType.MESH)

    for d in range(1, 8):
        greet(narrow_peer(d))
    greet(x_at(lax.rem(x + 2, 4)))
    greet(x_at(lax.rem(jnp.where(xl == 0, x + 3, x + 1), 4)))
    greet(sibling)

    @pl.when(is_mid)
    def _():
        for d in STEPS:
            greet(up(d))

    @pl.when(jnp.logical_not(is_mid))
    def _():
        greet(middle)

    is_root = jnp.logical_and(z == src_z, xh == 1)
    feeds = jnp.logical_or(is_src, is_root)
    is_fed = jnp.logical_and(is_mid, z != src_z)
    crosses = jnp.logical_and(z == 8, core == xh)
    across = dev(z, 1 - xh, 1 - core, 2 * y + 1 - xl)

    def fed_plane(k):
        return dev(lax.rem(z + 4 * k, 16), xh, owner, n)

    @pl.when(feeds)
    def _():
        for k in range(1, 4):
            greet(fed_plane(k))

    @pl.when(is_fed)
    def _():
        greet(dev(src_z, xh, core * xh, n))

    @pl.when(crosses)
    def _():
        greet(across)

    pl.semaphore_wait(
        barrier,
        10
        + jnp.where(is_mid, 3, 1)
        + jnp.where(feeds, 3, 0)
        + jnp.where(is_fed, 1, 0)
        + jnp.where(crosses, 1, 0),
    )

    def a_rows(yy, xx):
        return pl.ds(yy * 16 + xx * 4, 4)

    def b_rows(yy, xx):
        return pl.ds(64 + xx * 16 + yy * 4, 4)

    mine_a = own.at[a_rows(y, x)]
    mine_b = own.at[b_rows(y, x)]

    def owner_copies(i):
        rows = (a_rows, b_rows)[i]
        first = pan_in.at[pl.ds(i * 4, 4)]
        second = pan_in.at[pl.ds(8 + i * 4, 4)]
        here = own.at[rows(y, xl)]
        there = own.at[rows(y, 3 - xl)]
        root = dev(z, 1, owner, 2 * y + 1 - xl)
        return (
            [remote(second, there, a_send.at[i, 0], a_recv.at[i], root)]
            + [remote(first, here, a_send.at[i, k], a_recv.at[i], fed_plane(k)) for k in (2, 1, 3)],
            pltpu.make_async_copy(first, here, a_recv.at[i]),
            remote(first, here, a_send.at[i, 4], a_recv.at[i], sibling),
        )

    @pl.when(is_src)
    def _():
        for i in range(2):
            far, local, near = owner_copies(i)
            for c in far:
                c.start()

            @pl.when(owner == 0)
            def _():
                local.start()

            @pl.when(owner == 1)
            def _():
                near.start()

    def first_round(i, d):
        mine = (mine_a, mine_b)[i]
        if i == 0:
            to, came = x_at(lax.rem(x + d, 4)), own.at[a_rows(y, lax.rem(x + 4 - d, 4))]
        else:
            to, came = y_at(lax.rem(y + d, 4)), own.at[b_rows(lax.rem(y + 4 - d, 4), x)]
        sems = b1_send.at[i, d], b1_recv.at[i, d], to
        return remote(mine, mine, *sems), remote(came, came, *sems)

    def pass_on():
        for i, mine in enumerate((mine_a, mine_b)):
            remote(mine, mine, a_send.at[i, 0], a_recv.at[i], sibling).wait_recv()

            @pl.when(is_root)
            def _():
                for k in (2, 1, 3):
                    remote(mine, mine, a_send.at[i, k], a_recv.at[i], fed_plane(k)).start()

            @pl.when(is_mid)
            def _():
                for k, d in enumerate(STEPS):
                    remote(mine, mine, f_send.at[i, k], a_recv.at[i], up(d)).start()

            for d in (2, 1, 3):
                first_round(i, d)[0].start()

    @pl.when(is_mid)
    def _():
        pass_on()

    m = jnp.broadcast_to(imap[...], (8, ROWS))
    m = jnp.where(iota((8, ROWS), 0) == 0, lax.shift_right_logical(m, 7), jnp.bitwise_and(m, 127)).astype(F32).astype(BF16)
    lane = iota((128, 128), 1)
    row_of = (lane // 64) * 64 + jnp.bitwise_and(lane, 31) * 2 + jnp.bitwise_and(lane // 32, 1)
    swap = jnp.where(iota((128, 128), 0) == row_of, 1.0, 0.0).astype(BF16)
    tri = jnp.where(iota((128, 128), 0) < iota((128, 128), 1), 1.0, 0.0).astype(BF16)
    carry = jnp.zeros((8, 1), F32)
    idx_parts, spot_parts = [], []
    for b in range(8):
        t = jnp.dot(m[:, b * 128 : (b + 1) * 128], swap, preferred_element_type=F32).astype(jnp.int32)
        mb = t[0:1] * 128 + t[1:2]
        tb = lax.shift_right_logical(mb, 10)
        spot_parts.append(jnp.bitwise_and(mb, 1023) + 1)
        near = 2 * jnp.bitwise_and(lax.shift_right_logical(tb, 1) + 4 - y, 3) + jnp.bitwise_and(tb + xl, 1)
        hit = jnp.where(iota((8, 128), 0) == jnp.broadcast_to(tb, (8, 128)), 1.0, 0.0)
        before = jnp.dot(hit.astype(BF16), tri, preferred_element_type=F32) + carry
        carry = carry + jnp.sum(hit, axis=1, keepdims=True)
        rank = jnp.sum(hit * before, axis=0, keepdims=True)
        idx_parts.append(near * CAP + rank.astype(jnp.int32))
    idx = jnp.concatenate(idx_parts, axis=1)
    spot8 = jnp.broadcast_to(jnp.concatenate(spot_parts, axis=1), (8, ROWS))
    hi = lax.shift_right_logical(spot8, 5)
    lo = jnp.bitwise_and(spot8, 31)
    two = jnp.where(iota((8, ROWS), 0) == 0, hi, lo).astype(F32).astype(BF16)

    def build(g, _):
        rows = pl.ds(pl.multiple_of(g * CAP, CAP), CAP)
        s = jnp.where(iota((CAP, ROWS), 0) + g * CAP == idx, 1.0, 0.0).astype(BF16)
        sel[rows, :] = s
        t = lax.dot_general(two, s, (((1,), (1,)), ((), ())), preferred_element_type=F32)
        pos_s[g] = t
        return 0

    lax.fori_loop(0, 8, build, 0)

    pos_out = []
    for d in range(1, 8):
        c = remote(pos_s.at[d], pos_r.at[d], p_send.at[d], p_recv.at[d], narrow_peer(d))
        c.start()
        pos_out.append(c)
    pos_r[0] = pos_s[0]

    loads[2].wait()

    def flip(k, _):
        o = pl.ds(pl.multiple_of(k * 256, 256), 256)
        vt[:, o] = vx[o, :].T
        return 0

    lax.fori_loop(0, 4, flip, 0)
    br = brow[...]
    bc = bcol[...]
    sq = (SLOTS, SLOTS)
    diag = iota(sq, 0) == iota(sq, 1)
    br_b = jnp.broadcast_to(br, sq)
    brc = jnp.sum(jnp.where(diag, br_b, 0), axis=1, keepdims=True)
    bcc = jnp.sum(jnp.where(diag, jnp.broadcast_to(bc, sq), 0), axis=1, keepdims=True)
    earlier = jnp.logical_and(iota(sq, 0) < iota(sq, 1), brc == br_b)
    rank = jnp.sum(jnp.where(earlier, 1, 0), axis=0, keepdims=True)
    same = iota((RB, SLOTS), 0) == jnp.broadcast_to(br, (RB, SLOTS))
    count = jnp.sum(jnp.where(same, 1, 0), axis=1, keepdims=True)
    padded = jnp.bitwise_and(count + 3, -4)
    off = jnp.sum(jnp.where(iota((RB, SLOTS), 0) < br, padded, 0), axis=0, keepdims=True)
    dest = jnp.where(br < RB, off + rank, 4096)
    destc = jnp.sum(jnp.where(diag, jnp.broadcast_to(dest, sq), 0), axis=1, keepdims=True)
    count_l = jnp.sum(jnp.where(brc == iota((SLOTS, 128), 1), 1, 0), axis=0, keepdims=True)
    padded_l = jnp.bitwise_and(count_l + 3, -4)
    off_c = jnp.sum(jnp.where(iota((RB, 128), 1) < iota((RB, 128), 0), padded_l, 0), axis=1, keepdims=True)
    begins = jnp.logical_and(lax.shift_right_logical(off_c, 2) == iota((RB, 256), 1), count > 0)
    keep = 1 - jnp.sum(jnp.where(begins, 1, 0), axis=0, keepdims=True)
    end_l = jnp.sum(jnp.where(iota((RB, 256), 0) <= iota((RB, 256), 1), padded, 0), axis=0, keepdims=True)
    last = jnp.maximum(lax.shift_right_logical(end_l, 2) - 1, 0)
    some = jnp.minimum(count_l, 1)
    some = jnp.concatenate([some, some], axis=1)
    q = jnp.bitwise_and(bcc, 3)
    part = jnp.bitwise_and(lax.shift_right_logical(bcc, 2), 1)
    bxl = jnp.bitwise_and(lax.shift_right_logical(bcc, 4), 1)
    bx = jnp.where(jnp.bitwise_and(bcc, 8) == 8, 3 - bxl, bxl)
    by = lax.shift_right_logical(bcc, 5)
    place = jnp.where(part == 1, 64 + bx * 16 + by * 4, by * 16 + bx * 4) + q
    block = jnp.sum(jnp.where(destc == iota((SLOTS, 256), 1), place, 0), axis=0, keepdims=True)
    r8 = iota((8, 256), 0)
    meta[...] = jnp.where(r8 == 0, block, jnp.where(r8 == 1, keep, jnp.where(r8 == 2, last, some)))
    to_scalar = pltpu.make_async_copy(meta, meta_s, meta_sem)
    to_scalar.start()
    perm[...] = jnp.where(iota((SORTED, SLOTS), 0) == dest, 1.0, 0.0).astype(BF16)

    loads[0].wait()
    loads[1].wait()

    def order(j, _):
        lanes = pl.ds(pl.multiple_of(j * 512, 512), 512)
        for src, dst in ((kx, zk), (mx, zm)):
            t = jnp.dot(perm[...], src[:, lanes], preferred_element_type=F32)
            for i in range(4):
                dst[pl.ds(j * 4 + i, SORTED, stride=32), :] = t[:, i * 128 : (i + 1) * 128]
        return 0

    lax.fori_loop(0, 8, order, 0)
    @pl.when(jnp.logical_not(is_mid))
    def _():
        pass_on()

    row_a = own.at[pl.ds(y * 16, 16)]
    row_b = own.at[pl.ds(64 + x * 16, 16)]
    far_a = other.at[pl.ds(y * 16, 16)]
    far_b = other.at[pl.ds(64 + x * 16, 16)]
    b2_out, b2_in, c_out = [], [], []
    for i in range(2):
        block_ref = (row_a, row_b)[i]
        for d in (2, 1, 3):
            first_round(i, d)[1].wait_recv()
        for d in (2, 1, 3):
            if i == 0:
                to, o = y_at(lax.rem(y + d, 4)), lax.rem(y + 4 - d, 4) * 16
            else:
                to, o = x_at(lax.rem(x + d, 4)), 64 + lax.rem(x + 4 - d, 4) * 16
            c = remote(block_ref, block_ref, b2_send.at[i, d], b2_recv.at[i, d], to)
            c.start()
            b2_out.append(c)
            came = own.at[pl.ds(o, 16)]
            b2_in.append((came, o, d, remote(came, came, b2_send.at[i, d], b2_recv.at[i, d], to)))
        c = remote(block_ref, (far_a, far_b)[i], c_send.at[i], c_recv.at[i], sibling)
        c.start()
        c_out.append(c)

    left = iota((32, 128), 1) < 64

    def assemble(g, _):
        for mat, src in enumerate((zk, zm)):
            for pair in range(2):
                o = pl.multiple_of(g * 128 + pair * 64, 64)
                t0 = src[pl.ds(o, 32), :]
                t1 = src[pl.ds(o + 32, 32), :]
                even = jnp.where(left, t0, pltpu.roll(t1, 64, 1))
                odd = jnp.where(left, pltpu.roll(t0, 64, 1), t1)
                lhs[g, mat * 64 : mat * 64 + 32, pair * 128 : (pair + 1) * 128] = even.astype(BF16)
                lhs[g, mat * 64 + 32 : mat * 64 + 64, pair * 128 : (pair + 1) * 128] = odd.astype(BF16)
        return 0

    def assemble4(g4, _):
        for u in range(4):
            assemble(g4 * 4 + u, 0)
        return 0

    lax.fori_loop(0, GROUPS // 4, assemble4, 0)

    for k, (came, o, d, c) in enumerate(b2_in):
        c.wait_recv()
        h = remote(came, other.at[pl.ds(o, 16)], c_send.at[2 + k], c_recv.at[2 + k], sibling)
        h.start()
        c_out.append(h)
    to_scalar.wait()

    x_out = []
    for half in range(2):
        pan = (own, other)[half]
        if half == 1:
            offs = [y * 16, 64 + x * 16] + [o for _, o, _, _ in b2_in]
            for k, o in enumerate(offs):
                came = other.at[pl.ds(o, 16)]
                remote(came, came, c_send.at[k], c_recv.at[k], sibling).wait_recv()

        def multiply(g4, held):
            for u in range(13):
                g = g4 * 13 + u
                rhs = jnp.concatenate([pan[meta_s[0, g * 4 + i]] for i in range(4)], axis=0)
                t = jnp.dot(lhs[g], rhs, preferred_element_type=F32)
                held = t + held * meta_s[1, g].astype(F32)
                run[g] = held
            return held

        lax.fori_loop(0, GROUPS // 13, multiply, jnp.zeros((128, PC), F32))

        def collect(r, _):
            t = run[meta_s[2, r]] * meta_s[3, r].astype(F32)
            rows = pl.ds(r * BLK, BLK)
            prod[rows, 0:PC] = t[0:BLK].astype(BF16)
            prod[rows, PC : 2 * PC] = t[BLK : 2 * BLK].astype(BF16)
            return 0

        for r in range(RB):
            collect(r, 0)

        for first in (0, 4):
            rows = pl.ds(first * CAP, 4 * CAP)
            t = jnp.dot(sel[rows, :], prod[...], preferred_element_type=F32).astype(BF16)
            for d in range(first, first + 4):
                td = t[(d - first) * CAP : (d - first + 1) * CAP]
                if d == 0:
                    recv[half, 0:CAP, :] = td
                else:
                    send[half, d] = td
                    c = remote(
                        send.at[half, d], recv.at[half, d * CAP : (d + 1) * CAP],
                        x_send.at[half, d], x_recv.at[half, d], narrow_peer(d),
                    )
                    c.start()
                    x_out.append(c)

    for d in range(1, 8):
        pos_out[d - 1].wait_recv()

    def weigh(d, _):
        t = pos_r[d]
        at = (t[0:1, :] * 32.0 + t[1:2, :]).astype(jnp.int32)
        q_d = jnp.where(iota((ROWS, CAP), 0) + 1 == at, 1.0, 0.0).astype(BF16)
        wts[:, pl.ds(pl.multiple_of(d * CAP, CAP), CAP)] = jnp.dot(
            vt[...], q_d, preferred_element_type=F32
        ).astype(BF16)
        return 0

    lax.fori_loop(0, 8, weigh, 0)

    for half in range(2):
        which = core if half == 0 else 1 - core
        for c in x_out[half * 7 : half * 7 + 7]:
            c.wait_recv()
        t = jnp.dot(wts[...], recv[half], preferred_element_type=F32)
        out[:, pl.ds(pl.multiple_of(which * 2 * PC, 2 * PC), 2 * PC)] = t.astype(BF16)

    for i in range(2):
        for d in (2, 1, 3):
            first_round(i, d)[0].wait_send()
    for c in pos_out + b2_out + c_out + x_out:
        c.wait_send()

    @pl.when(is_mid)
    def _():
        for i, mine in enumerate((mine_a, mine_b)):
            for k, d in enumerate(STEPS):
                remote(mine, mine, f_send.at[i, k], a_recv.at[i], up(d)).wait_send()

    @pl.when(is_root)
    def _():
        for i, mine in enumerate((mine_a, mine_b)):
            for k in (2, 1, 3):
                remote(mine, mine, a_send.at[i, k], a_recv.at[i], fed_plane(k)).wait_send()

    @pl.when(is_src)
    def _():
        for i in range(2):
            far, local, near = owner_copies(i)
            for c in far:
                c.wait_send()

            @pl.when(owner == 1)
            def _():
                near.wait_send()


def body(panels, stiff_blocks, mass_blocks, block_rows, block_cols, interface_map, cond_vectors):
    hbm = pl.BlockSpec(memory_space=pl.ANY)
    vmem = pl.BlockSpec(memory_space=pltpu.VMEM)
    dma = pltpu.SemaphoreType.DMA
    res = pl.pallas_call(
        kernel,
        out_shape=jax.ShapeDtypeStruct((NC, 4 * PC), BF16),
        in_specs=[hbm, hbm, hbm, vmem, vmem, vmem, hbm],
        out_specs=vmem,
        scratch_shapes=[
            pltpu.VMEM((128, BLK, PC), BF16),
            pltpu.VMEM((128, BLK, PC), BF16),
            pltpu.VMEM((SLOTS, BLK * BLK), BF16),
            pltpu.VMEM((SLOTS, BLK * BLK), BF16),
            pltpu.VMEM((ROWS, NC), BF16),
            pltpu.VMEM((NC, ROWS), BF16),
            pltpu.VMEM((SORTED, SLOTS), BF16),
            pltpu.VMEM((SORTED * 32, 128), F32),
            pltpu.VMEM((SORTED * 32, 128), F32),
            pltpu.VMEM((GROUPS, 128, 256), BF16),
            pltpu.VMEM((GROUPS, 128, PC), F32),
            pltpu.VMEM((ROWS, 2 * PC), BF16),
            pltpu.VMEM((8 * CAP, ROWS), BF16),
            pltpu.VMEM((NC, 8 * CAP), BF16),
            pltpu.VMEM((8, 8, CAP), F32),
            pltpu.VMEM((8, 8, CAP), F32),
            pltpu.VMEM((2, 8, CAP, 2 * PC), BF16),
            pltpu.VMEM((2, 8 * CAP, 2 * PC), BF16),
            pltpu.VMEM((8, 256), jnp.int32),
            pltpu.SMEM((8, 256), jnp.int32),
            dma((3,)), dma, dma((2, 8)), dma((2,)), dma((2, 3)), dma((2, 4)), dma((2, 4)), dma((2, 4)), dma((2, 4)),
            dma((8,)), dma((8,)), dma((8,)), dma((8,)), dma((2, 8)), dma((2, 8)),
        ],
        compiler_params=pltpu.CompilerParams(
            collective_id=0, has_side_effects=True, vmem_limit_bytes=60 * 2**20
        ),
    )(panels.reshape(RB, BLK, PC), stiff_blocks, mass_blocks, block_rows, block_cols, interface_map, cond_vectors)
    return res.reshape(1, 1, NC, 4 * PC)


def solution(mesh):
    return jax.shard_map(
        body,
        mesh=mesh,
        in_specs=(
            P("wide", "narrow", None),
            P("wide", "narrow", None),
            P("wide", "narrow", None),
            P("wide", "narrow"),
            P("wide", "narrow"),
            P("wide", "narrow"),
            P("narrow", None),
        ),
        out_specs=P("wide", "narrow", None, None),
        check_vma=False,
    )
```

```python
import jax
import jax.numpy as jnp
from jax import lax
from jax.experimental import pallas as pl
from jax.experimental.pallas import tpu as pltpu
from jax.sharding import PartitionSpec as P

BLK = 64
PC = 128
NC = 768
RB = 16
SLOTS = 152
ROWS = 1024
CAP = 256
GROUPS = 52
SORTED = GROUPS * 4
F32 = jnp.float32
BF16 = jnp.bfloat16


def iota(shape, dim):
    return lax.broadcasted_iota(jnp.int32, shape, dim)


def kernel(
    pan_in, stiff, mass, brow, bcol, imap, vec, out,
    own, other, kx, mx, vx, vt, perm, zk, zm, lhs, run, prod, sel, wts, pos_s, pos_r, send, recv,
    meta, meta_s,
    load_sem, meta_sem, a_send, a_recv, f_send, b1_send, b1_recv, b2_send, b2_recv,
    c_send, c_recv, p_send, p_recv, x_send, x_recv,
):
    w = lax.axis_index("wide")
    n = lax.axis_index("narrow")
    core = lax.rem(w, 2)
    xh = lax.rem(w // 2, 2)
    z = w // 4
    y = n // 2
    xl = lax.rem(n, 2)
    x = 2 * xh + xl

    def dev(z_, xh_, core_, n_):
        return {"wide": z_ * 4 + xh_ * 2 + core_, "narrow": n_}

    def remote(src, dst, ssem, rsem, where):
        return pltpu.make_async_remote_copy(
            src_ref=src, dst_ref=dst, send_sem=ssem, recv_sem=rsem,
            device_id=where, device_id_type=pl.DeviceIdType.MESH,
        )

    loads = [
        pltpu.make_async_copy(stiff.at[0], kx, load_sem.at[0]),
        pltpu.make_async_copy(mass.at[0], mx, load_sem.at[1]),
        pltpu.make_async_copy(vec, vx, load_sem.at[2]),
    ]
    for c in loads:
        c.start()

    def narrow_peer(d):
        return dev(z, xh, core, lax.rem(y + d // 2, 4) * 2 + lax.rem(xl + d % 2, 2))

    def x_at(xx):
        return dev(z, xx // 2, core, y * 2 + lax.rem(xx, 2))

    def y_at(yy):
        return dev(z, xh, core, yy * 2 + xl)

    sibling = dev(z, xh, 1 - core, n)
    zm4 = lax.rem(z, 4)
    is_mid = zm4 == 0
    owner = z // 8
    is_src = jnp.logical_and(lax.rem(z, 8) == 0, jnp.logical_and(xh == 0, core == 0))
    src_z = 8 * core

    def up(d):
        return dev(lax.rem(z + 16 + d, 16), xh, core, n)

    STEPS = (2, 1, -1)
    middle = dev(lax.rem(jnp.where(zm4 == 3, z + 1, z - zm4), 16), xh, core, n)

    barrier = pltpu.get_barrier_semaphore()

    def greet(where):
        pl.semaphore_signal(barrier, inc=1, device_id=where, device_id_type=pl.DeviceIdType.MESH)

    for d in range(1, 8):
        greet(narrow_peer(d))
    greet(x_at(lax.rem(x + 2, 4)))
    greet(x_at(lax.rem(jnp.where(xl == 0, x + 3, x + 1), 4)))
    greet(sibling)

    @pl.when(is_mid)
    def _():
        for d in STEPS:
            greet(up(d))

    @pl.when(jnp.logical_not(is_mid))
    def _():
        greet(middle)

    is_root = jnp.logical_and(z == src_z, xh == 1)
    feeds = jnp.logical_or(is_src, is_root)
    is_fed = jnp.logical_and(is_mid, z != src_z)
    crosses = jnp.logical_and(z == 8, core == xh)
    across = dev(z, 1 - xh, 1 - core, 2 * y + 1 - xl)

    def fed_plane(k):
        return dev(lax.rem(z + 4 * k, 16), xh, owner, n)

    @pl.when(feeds)
    def _():
        for k in range(1, 4):
            greet(fed_plane(k))

    @pl.when(is_fed)
    def _():
        greet(dev(src_z, xh, core * xh, n))

    @pl.when(crosses)
    def _():
        greet(across)

    pl.semaphore_wait(
        barrier,
        10
        + jnp.where(is_mid, 3, 1)
        + jnp.where(feeds, 3, 0)
        + jnp.where(is_fed, 1, 0)
        + jnp.where(crosses, 1, 0),
    )

    def a_rows(yy, xx):
        return pl.ds(yy * 16 + xx * 4, 4)

    def b_rows(yy, xx):
        return pl.ds(64 + xx * 16 + yy * 4, 4)

    mine_a = own.at[a_rows(y, x)]
    mine_b = own.at[b_rows(y, x)]

    def owner_copies(i):
        rows = (a_rows, b_rows)[i]
        first = pan_in.at[pl.ds(i * 4, 4)]
        second = pan_in.at[pl.ds(8 + i * 4, 4)]
        here = own.at[rows(y, xl)]
        there = own.at[rows(y, 3 - xl)]
        root = dev(z, 1, owner, 2 * y + 1 - xl)
        return (
            [remote(second, there, a_send.at[i, 0], a_recv.at[i], root)]
            + [remote(first, here, a_send.at[i, k], a_recv.at[i], fed_plane(k)) for k in (2, 1, 3)],
            pltpu.make_async_copy(first, here, a_recv.at[i]),
            remote(first, here, a_send.at[i, 4], a_recv.at[i], sibling),
        )

    @pl.when(is_src)
    def _():
        for i in range(2):
            far, local, near = owner_copies(i)
            for c in far:
                c.start()

            @pl.when(owner == 0)
            def _():
                local.start()

            @pl.when(owner == 1)
            def _():
                near.start()

    def first_round(i, d):
        mine = (mine_a, mine_b)[i]
        if i == 0:
            to, came = x_at(lax.rem(x + d, 4)), own.at[a_rows(y, lax.rem(x + 4 - d, 4))]
        else:
            to, came = y_at(lax.rem(y + d, 4)), own.at[b_rows(lax.rem(y + 4 - d, 4), x)]
        sems = b1_send.at[i, d], b1_recv.at[i, d], to
        return remote(mine, mine, *sems), remote(came, came, *sems)

    def pass_on():
        for i, mine in enumerate((mine_a, mine_b)):
            remote(mine, mine, a_send.at[i, 0], a_recv.at[i], sibling).wait_recv()

            @pl.when(is_root)
            def _():
                for k in (2, 1, 3):
                    remote(mine, mine, a_send.at[i, k], a_recv.at[i], fed_plane(k)).start()

            @pl.when(is_mid)
            def _():
                for k, d in enumerate(STEPS):
                    remote(mine, mine, f_send.at[i, k], a_recv.at[i], up(d)).start()

            for d in (2, 1, 3):
                first_round(i, d)[0].start()

    @pl.when(is_mid)
    def _():
        pass_on()

    m = jnp.broadcast_to(imap[...], (8, ROWS))
    m = jnp.where(iota((8, ROWS), 0) == 0, lax.shift_right_logical(m, 7), jnp.bitwise_and(m, 127)).astype(F32).astype(BF16)
    lane = iota((128, 128), 1)
    row_of = (lane // 64) * 64 + jnp.bitwise_and(lane, 31) * 2 + jnp.bitwise_and(lane // 32, 1)
    swap = jnp.where(iota((128, 128), 0) == row_of, 1.0, 0.0).astype(BF16)
    tri = jnp.where(iota((128, 128), 0) < iota((128, 128), 1), 1.0, 0.0).astype(BF16)
    carry = jnp.zeros((8, 1), F32)
    idx_parts, spot_parts = [], []
    for b in range(8):
        t = jnp.dot(m[:, b * 128 : (b + 1) * 128], swap, preferred_element_type=F32).astype(jnp.int32)
        mb = t[0:1] * 128 + t[1:2]
        tb = lax.shift_right_logical(mb, 10)
        spot_parts.append(jnp.bitwise_and(mb, 1023) + 1)
        near = 2 * jnp.bitwise_and(lax.shift_right_logical(tb, 1) + 4 - y, 3) + jnp.bitwise_and(tb + xl, 1)
        hit = jnp.where(iota((8, 128), 0) == jnp.broadcast_to(tb, (8, 128)), 1.0, 0.0)
        before = jnp.dot(hit.astype(BF16), tri, preferred_element_type=F32) + carry
        carry = carry + jnp.sum(hit, axis=1, keepdims=True)
        rank = jnp.sum(hit * before, axis=0, keepdims=True)
        idx_parts.append(near * CAP + rank.astype(jnp.int32))
    idx = jnp.concatenate(idx_parts, axis=1)
    spot8 = jnp.broadcast_to(jnp.concatenate(spot_parts, axis=1), (8, ROWS))
    hi = lax.shift_right_logical(spot8, 5)
    lo = jnp.bitwise_and(spot8, 31)
    two = jnp.where(iota((8, ROWS), 0) == 0, hi, lo).astype(F32).astype(BF16)

    def build(g, _):
        rows = pl.ds(pl.multiple_of(g * CAP, CAP), CAP)
        s = jnp.where(iota((CAP, ROWS), 0) + g * CAP == idx, 1.0, 0.0).astype(BF16)
        sel[rows, :] = s
        t = lax.dot_general(two, s, (((1,), (1,)), ((), ())), preferred_element_type=F32)
        pos_s[g] = t
        return 0

    lax.fori_loop(0, 8, build, 0)

    pos_out = []
    for d in range(1, 8):
        c = remote(pos_s.at[d], pos_r.at[d], p_send.at[d], p_recv.at[d], narrow_peer(d))
        c.start()
        pos_out.append(c)
    pos_r[0] = pos_s[0]

    loads[2].wait()

    def flip(k, _):
        o = pl.ds(pl.multiple_of(k * 256, 256), 256)
        vt[:, o] = vx[o, :].T
        return 0

    lax.fori_loop(0, 4, flip, 0)
    br = brow[...]
    bc = bcol[...]
    sq = (SLOTS, SLOTS)
    diag = iota(sq, 0) == iota(sq, 1)
    br_b = jnp.broadcast_to(br, sq)
    brc = jnp.sum(jnp.where(diag, br_b, 0), axis=1, keepdims=True)
    bcc = jnp.sum(jnp.where(diag, jnp.broadcast_to(bc, sq), 0), axis=1, keepdims=True)
    earlier = jnp.logical_and(iota(sq, 0) < iota(sq, 1), brc == br_b)
    rank = jnp.sum(jnp.where(earlier, 1, 0), axis=0, keepdims=True)
    same = iota((RB, SLOTS), 0) == jnp.broadcast_to(br, (RB, SLOTS))
    count = jnp.sum(jnp.where(same, 1, 0), axis=1, keepdims=True)
    padded = jnp.bitwise_and(count + 3, -4)
    off = jnp.sum(jnp.where(iota((RB, SLOTS), 0) < br, padded, 0), axis=0, keepdims=True)
    dest = jnp.where(br < RB, off + rank, 4096)
    destc = jnp.sum(jnp.where(diag, jnp.broadcast_to(dest, sq), 0), axis=1, keepdims=True)
    count_l = jnp.sum(jnp.where(brc == iota((SLOTS, 128), 1), 1, 0), axis=0, keepdims=True)
    padded_l = jnp.bitwise_and(count_l + 3, -4)
    off_c = jnp.sum(jnp.where(iota((RB, 128), 1) < iota((RB, 128), 0), padded_l, 0), axis=1, keepdims=True)
    begins = jnp.logical_and(lax.shift_right_logical(off_c, 2) == iota((RB, 256), 1), count > 0)
    keep = 1 - jnp.sum(jnp.where(begins, 1, 0), axis=0, keepdims=True)
    end_l = jnp.sum(jnp.where(iota((RB, 256), 0) <= iota((RB, 256), 1), padded, 0), axis=0, keepdims=True)
    last = jnp.maximum(lax.shift_right_logical(end_l, 2) - 1, 0)
    some = jnp.minimum(count_l, 1)
    some = jnp.concatenate([some, some], axis=1)
    q = jnp.bitwise_and(bcc, 3)
    part = jnp.bitwise_and(lax.shift_right_logical(bcc, 2), 1)
    bxl = jnp.bitwise_and(lax.shift_right_logical(bcc, 4), 1)
    bx = jnp.where(jnp.bitwise_and(bcc, 8) == 8, 3 - bxl, bxl)
    by = lax.shift_right_logical(bcc, 5)
    place = jnp.where(part == 1, 64 + bx * 16 + by * 4, by * 16 + bx * 4) + q
    block = jnp.sum(jnp.where(destc == iota((SLOTS, 256), 1), place, 0), axis=0, keepdims=True)
    r8 = iota((8, 256), 0)
    meta[...] = jnp.where(r8 == 0, block, jnp.where(r8 == 1, keep, jnp.where(r8 == 2, last, some)))
    to_scalar = pltpu.make_async_copy(meta, meta_s, meta_sem)
    to_scalar.start()
    perm[...] = jnp.where(iota((SORTED, SLOTS), 0) == dest, 1.0, 0.0).astype(BF16)

    loads[0].wait()
    loads[1].wait()

    def order(j, _):
        lanes = pl.ds(pl.multiple_of(j * 512, 512), 512)
        for src, dst in ((kx, zk), (mx, zm)):
            t = jnp.dot(perm[...], src[:, lanes], preferred_element_type=F32)
            for i in range(4):
                dst[pl.ds(j * 4 + i, SORTED, stride=32), :] = t[:, i * 128 : (i + 1) * 128]
        return 0

    lax.fori_loop(0, 8, order, 0)
    @pl.when(jnp.logical_not(is_mid))
    def _():
        pass_on()

    row_a = own.at[pl.ds(y * 16, 16)]
    row_b = own.at[pl.ds(64 + x * 16, 16)]
    far_a = other.at[pl.ds(y * 16, 16)]
    far_b = other.at[pl.ds(64 + x * 16, 16)]
    b2_out, b2_in, c_out = [], [], []
    for i in range(2):
        block_ref = (row_a, row_b)[i]
        for d in (2, 1, 3):
            first_round(i, d)[1].wait_recv()
        for d in (2, 1, 3):
            if i == 0:
                to, o = y_at(lax.rem(y + d, 4)), lax.rem(y + 4 - d, 4) * 16
            else:
                to, o = x_at(lax.rem(x + d, 4)), 64 + lax.rem(x + 4 - d, 4) * 16
            c = remote(block_ref, block_ref, b2_send.at[i, d], b2_recv.at[i, d], to)
            c.start()
            b2_out.append(c)
            came = own.at[pl.ds(o, 16)]
            b2_in.append((came, o, d, remote(came, came, b2_send.at[i, d], b2_recv.at[i, d], to)))
        c = remote(block_ref, (far_a, far_b)[i], c_send.at[i], c_recv.at[i], sibling)
        c.start()
        c_out.append(c)

    left = iota((32, 128), 1) < 64

    def assemble(g, _):
        for mat, src in enumerate((zk, zm)):
            for pair in range(2):
                o = pl.multiple_of(g * 128 + pair * 64, 64)
                t0 = src[pl.ds(o, 32), :]
                t1 = src[pl.ds(o + 32, 32), :]
                even = jnp.where(left, t0, pltpu.roll(t1, 64, 1))
                odd = jnp.where(left, pltpu.roll(t0, 64, 1), t1)
                lhs[g, mat * 64 : mat * 64 + 32, pair * 128 : (pair + 1) * 128] = even.astype(BF16)
                lhs[g, mat * 64 + 32 : mat * 64 + 64, pair * 128 : (pair + 1) * 128] = odd.astype(BF16)
        return 0

    def assemble4(g4, _):
        for u in range(4):
            assemble(g4 * 4 + u, 0)
        return 0

    lax.fori_loop(0, GROUPS // 4, assemble4, 0)

    for k, (came, o, d, c) in enumerate(b2_in):
        c.wait_recv()
        h = remote(came, other.at[pl.ds(o, 16)], c_send.at[2 + k], c_recv.at[2 + k], sibling)
        h.start()
        c_out.append(h)
    to_scalar.wait()

    x_out = []
    for half in range(2):
        pan = (own, other)[half]
        if half == 1:
            offs = [y * 16, 64 + x * 16] + [o for _, o, _, _ in b2_in]
            for k, o in enumerate(offs):
                came = other.at[pl.ds(o, 16)]
                remote(came, came, c_send.at[k], c_recv.at[k], sibling).wait_recv()

        def multiply(g4, held):
            for u in range(26):
                g = g4 * 26 + u
                rhs = jnp.concatenate([pan[meta_s[0, g * 4 + i]] for i in range(4)], axis=0)
                t = jnp.dot(lhs[g], rhs, preferred_element_type=F32)
                held = t + held * meta_s[1, g].astype(F32)
                run[g] = held
            return held

        lax.fori_loop(0, GROUPS // 26, multiply, jnp.zeros((128, PC), F32))

        def collect(r, _):
            t = run[meta_s[2, r]] * meta_s[3, r].astype(F32)
            rows = pl.ds(r * BLK, BLK)
            prod[rows, 0:PC] = t[0:BLK].astype(BF16)
            prod[rows, PC : 2 * PC] = t[BLK : 2 * BLK].astype(BF16)
            return 0

        for r in range(RB):
            collect(r, 0)

        for first in (0, 2, 4, 6):
            rows = pl.ds(first * CAP, 2 * CAP)
            t = jnp.dot(sel[rows, :], prod[...], preferred_element_type=F32).astype(BF16)
            for d in range(first, first + 2):
                td = t[(d - first) * CAP : (d - first + 1) * CAP]
                if d == 0:
                    recv[half, 0:CAP, :] = td
                else:
                    send[half, d] = td
                    c = remote(
                        send.at[half, d], recv.at[half, d * CAP : (d + 1) * CAP],
                        x_send.at[half, d], x_recv.at[half, d], narrow_peer(d),
                    )
                    c.start()
                    x_out.append(c)

    for d in range(1, 8):
        pos_out[d - 1].wait_recv()

    def weigh(d, _):
        t = pos_r[d]
        at = (t[0:1, :] * 32.0 + t[1:2, :]).astype(jnp.int32)
        q_d = jnp.where(iota((ROWS, CAP), 0) + 1 == at, 1.0, 0.0).astype(BF16)
        wts[:, pl.ds(pl.multiple_of(d * CAP, CAP), CAP)] = jnp.dot(
            vt[...], q_d, preferred_element_type=F32
        ).astype(BF16)
        return 0

    lax.fori_loop(0, 8, weigh, 0)

    for half in range(2):
        which = core if half == 0 else 1 - core
        for c in x_out[half * 7 : half * 7 + 7]:
            c.wait_recv()
        t = jnp.dot(wts[...], recv[half], preferred_element_type=F32)
        out[:, pl.ds(pl.multiple_of(which * 2 * PC, 2 * PC), 2 * PC)] = t.astype(BF16)

    for i in range(2):
        for d in (2, 1, 3):
            first_round(i, d)[0].wait_send()
    for c in pos_out + b2_out + c_out + x_out:
        c.wait_send()

    @pl.when(is_mid)
    def _():
        for i, mine in enumerate((mine_a, mine_b)):
            for k, d in enumerate(STEPS):
                remote(mine, mine, f_send.at[i, k], a_recv.at[i], up(d)).wait_send()

    @pl.when(is_root)
    def _():
        for i, mine in enumerate((mine_a, mine_b)):
            for k in (2, 1, 3):
                remote(mine, mine, a_send.at[i, k], a_recv.at[i], fed_plane(k)).wait_send()

    @pl.when(is_src)
    def _():
        for i in range(2):
            far, local, near = owner_copies(i)
            for c in far:
                c.wait_send()

            @pl.when(owner == 1)
            def _():
                near.wait_send()


def body(panels, stiff_blocks, mass_blocks, block_rows, block_cols, interface_map, cond_vectors):
    hbm = pl.BlockSpec(memory_space=pl.ANY)
    vmem = pl.BlockSpec(memory_space=pltpu.VMEM)
    dma = pltpu.SemaphoreType.DMA
    res = pl.pallas_call(
        kernel,
        out_shape=jax.ShapeDtypeStruct((NC, 4 * PC), BF16),
        in_specs=[hbm, hbm, hbm, vmem, vmem, vmem, hbm],
        out_specs=vmem,
        scratch_shapes=[
            pltpu.VMEM((128, BLK, PC), BF16),
            pltpu.VMEM((128, BLK, PC), BF16),
            pltpu.VMEM((SLOTS, BLK * BLK), BF16),
            pltpu.VMEM((SLOTS, BLK * BLK), BF16),
            pltpu.VMEM((ROWS, NC), BF16),
            pltpu.VMEM((NC, ROWS), BF16),
            pltpu.VMEM((SORTED, SLOTS), BF16),
            pltpu.VMEM((SORTED * 32 + 32, 128), F32),
            pltpu.VMEM((SORTED * 32 + 32, 128), F32),
            pltpu.VMEM((GROUPS, 128, 256), BF16),
            pltpu.VMEM((GROUPS, 128, PC), F32),
            pltpu.VMEM((ROWS, 2 * PC), BF16),
            pltpu.VMEM((8 * CAP, ROWS), BF16),
            pltpu.VMEM((NC, 8 * CAP), BF16),
            pltpu.VMEM((8, 8, CAP), F32),
            pltpu.VMEM((8, 8, CAP), F32),
            pltpu.VMEM((2, 8, CAP, 2 * PC), BF16),
            pltpu.VMEM((2, 8 * CAP, 2 * PC), BF16),
            pltpu.VMEM((8, 256), jnp.int32),
            pltpu.SMEM((8, 256), jnp.int32),
            dma((3,)), dma, dma((2, 8)), dma((2,)), dma((2, 3)), dma((2, 4)), dma((2, 4)), dma((2, 4)), dma((2, 4)),
            dma((8,)), dma((8,)), dma((8,)), dma((8,)), dma((2, 8)), dma((2, 8)),
        ],
        compiler_params=pltpu.CompilerParams(
            collective_id=0, has_side_effects=True, vmem_limit_bytes=60 * 2**20
        ),
    )(panels.reshape(RB, BLK, PC), stiff_blocks, mass_blocks, block_rows, block_cols, interface_map, cond_vectors)
    return res.reshape(1, 1, NC, 4 * PC)


def solution(mesh):
    return jax.shard_map(
        body,
        mesh=mesh,
        in_specs=(
            P("wide", "narrow", None),
            P("wide", "narrow", None),
            P("wide", "narrow", None),
            P("wide", "narrow"),
            P("wide", "narrow"),
            P("wide", "narrow"),
            P("narrow", None),
        ),
        out_specs=P("wide", "narrow", None, None),
        check_vma=False,
    )
```
